32 devices in a mesh: groups: 2 (over y), wide: 4 (over z), narrow: 2 (over x), probe: 2 (over core).
Axes of the slice: x: 2, y: 2, z: 4, core: 2. Of those that a mesh axis runs over, the one named last changes fastest.
Arguments:
- object_slab: bfloat16 [2, 2560, 2048], P(None, ('groups', 'narrow'), 'wide'), parts along dimension 1, may hold values from -6 to 6
- probe_wave: bfloat16 [2, 512, 512], replicated, may hold values from -6 to 6
- amplitude: bfloat16 [4, 4, 2, 512, 512], P(('groups', 'narrow'), 'wide', 'probe'), parts along dimension 0, may hold values from 0.19921875 to 2.5
- row_offset: int32 [4, 4, 2], P(('groups', 'narrow'), 'wide', 'probe'), parts along dimension 0, may hold values from 0 to 639
- col_offset: int32 [4, 4, 2], P(('groups', 'narrow'), 'wide', 'probe'), parts along dimension 0, may hold values from 0 to 511
- occupied: int32 [4, 4, 2], P(('groups', 'narrow'), 'wide', 'probe'), parts along dimension 0, may hold values 0 or 1
Outputs:
- object_grad: bfloat16 [2, 2560, 2048], P(None, ('groups', 'narrow'), 'wide'), parts along dimension 1
- probe_grad: float32 [2, 1024, 512], P(None, ('groups', 'wide'), ('narrow', 'probe')), parts along dimension 1
The draws below stay inside these ranges and needn't reach their ends.
There are 2 independent parts, one for each index of `groups`. The reference program is written for one: setup_inputs(seed, part) draws one part's arguments, and reference() takes and returns one part's arrays. A program takes and returns all parts, laid end to end along the dimension named above; an argument that names none is the same for every part. Nothing has to cross between parts.
All inputs are finite; a program needn't handle non-finite values. No bound on the sum of `occupied` on one device may be relied on, other than what follows from the above.
Results may differ from the reference program's by a relative error of at most 0.0093.
Values may be sent and summed in bfloat16 or wider, within the bound.
No kernel may reach another device: no remote copies, remote signals or barrier semaphores. Data moves between devices by JAX's collectives and lax.ppermute only.
A program may use at most 128 MiB of HBM per device.

```python
import math
import jax
import jax.numpy as jnp
from jax import lax

P_SIZE = 512
TC = 512
TR = 640
NR = 1280
NC = 2048
N_WIDE = 4
N_NARROW = 2
N_PROBE = 2


def set_ends(array, rng, low, largest):
    longest = array.shape.index(max(array.shape))
    spots = []
    for shift in (0, 1):
        where = [jax.random.randint(jax.random.fold_in(rng, axis), (), 0, length) for axis, length in enumerate(array.shape)]
        where[longest] = (where[longest] + shift) % array.shape[longest]
        spots.append(tuple(where))
    return array.at[spots[0]].set(low).at[spots[1]].set(largest)


def block_levels(stream_key, shape, pieces, smallest, top_value):
    gain = 1.0
    for axis_at, blocks in pieces:
        draws = jax.random.uniform(jax.random.fold_in(jax.random.fold_in(stream_key, 6), axis_at), (blocks,), jnp.float32, smallest / len(pieces), top_value / len(pieces))
        gain = gain * jnp.repeat(jnp.exp(draws), shape[axis_at] // blocks).reshape((-1,) + (1,) * (len(shape) - 1 - axis_at))
    return gain


def normal_values(own_key, dims, spread, most, pieces=(), dtype=jnp.bfloat16):
    values = spread * jax.random.normal(own_key, dims, jnp.float32)
    if pieces:
        values = values * block_levels(own_key, dims, pieces, -0.22, 0.18)
    return jnp.clip(values, -most, most).astype(dtype)


def setup_inputs(seed: int = 0, part: int = 0) -> dict:
    seeds = jax.random.split(jax.random.key(seed), 7)
    own_keys = jax.random.split(jax.random.fold_in(seeds[6], part), 7)
    object_slab = normal_values(own_keys[0], (2, NR, NC), 1.0, 6.0, ((1, 2), (2, 4)))
    probe_wave = normal_values(seeds[1], (2, P_SIZE, P_SIZE), 1.0, 6.0)
    amplitude = jnp.clip(0.19921875 + 2.3007812 * jax.random.uniform(own_keys[2], (N_NARROW, N_WIDE, N_PROBE, P_SIZE, P_SIZE), jnp.float32) ** block_levels(own_keys[2], (N_NARROW, N_WIDE, N_PROBE, P_SIZE, P_SIZE), ((0, 2), (1, 4), (2, 2)), -0.2, 0.2), 0.19921875, 2.5).astype(jnp.bfloat16)
    row_offset = set_ends(jax.random.randint(own_keys[3], (N_NARROW, N_WIDE, N_PROBE), 0, TR), jax.random.fold_in(own_keys[3], 1), 0, TR - 1).astype(jnp.int32)
    col_offset = set_ends(jax.random.randint(own_keys[4], (N_NARROW, N_WIDE, N_PROBE), 0, TC), jax.random.fold_in(own_keys[4], 1), 0, TC - 1).astype(jnp.int32)
    occupied = set_ends((jax.random.randint(own_keys[5], (N_NARROW, N_WIDE, N_PROBE), 0, 4) < 3).astype(jnp.int32), jax.random.fold_in(own_keys[5], 1), 0, 1)
    return {"object_slab": object_slab, "probe_wave": probe_wave, "amplitude": amplitude, "row_offset": row_offset, "col_offset": col_offset, "occupied": occupied}


def dft_tables(size):
    index = jnp.arange(size).astype(jnp.int32)
    product = index[:, None] * index[None, :] % size
    angle = product.astype(jnp.float32) * (2.0 * math.pi / size)
    norm = 1.0 / math.sqrt(size)
    return ((jnp.cos(angle) * norm).astype(jnp.bfloat16), (-jnp.sin(angle) * norm).astype(jnp.bfloat16))

def stacked(cos_part, sin_part):
    right_side = jnp.concatenate([jnp.concatenate([cos_part, sin_part], 1), jnp.concatenate([-sin_part, cos_part], 1)], 0)
    left_side = jnp.concatenate([jnp.concatenate([cos_part, -sin_part], 1), jnp.concatenate([sin_part, cos_part], 1)], 0)
    return (right_side, left_side)

def transform(real_part, imag_part, right_side, left_side):
    size = real_part.shape[0]
    halves = jnp.dot(jnp.concatenate([real_part, imag_part], 1), right_side, preferred_element_type=jnp.float32).astype(jnp.bfloat16)
    joined = jnp.concatenate([halves[:, :size], halves[:, size:]], 0)
    result = jnp.dot(left_side, joined, preferred_element_type=jnp.float32)
    return (result[:size], result[size:])

def position_terms(patch, probe_wave, amp_block, live, tables):
    fwd_right, fwd_left, inv_right, inv_left = tables
    probe_re = probe_wave[0].astype(jnp.float32)
    probe_im = probe_wave[1].astype(jnp.float32)
    patch_re = patch[0].astype(jnp.float32)
    patch_im = patch[1].astype(jnp.float32)
    exit_re = (probe_re * patch_re - probe_im * patch_im).astype(jnp.bfloat16)
    exit_im = (probe_re * patch_im + probe_im * patch_re).astype(jnp.bfloat16)
    far_re, far_im = transform(exit_re, exit_im, fwd_right, fwd_left)
    magnitude = jnp.sqrt(far_re * far_re + far_im * far_im)
    factor = (1.0 - amp_block.astype(jnp.float32) / jnp.maximum(magnitude, 1.0)) * live
    chi_re = (far_re * factor).astype(jnp.bfloat16)
    chi_im = (far_im * factor).astype(jnp.bfloat16)
    back_re, back_im = transform(chi_re, chi_im, inv_right, inv_left)
    obj_term = jnp.stack([probe_re * back_re + probe_im * back_im, probe_re * back_im - probe_im * back_re])
    probe_term = jnp.stack([patch_re * back_re + patch_im * back_im, patch_re * back_im - patch_im * back_re])
    return (obj_term, probe_term)

def make_tables(size):
    cos_part, sin_part = dft_tables(size)
    fwd_right, fwd_left = stacked(cos_part, sin_part)
    inv_right, inv_left = stacked(cos_part, -sin_part)
    return (fwd_right, fwd_left, inv_right, inv_left)

def reference(object_slab, probe_wave, amplitude, row_offset, col_offset, occupied):
    tables = make_tables(P_SIZE)
    padded = jnp.pad(object_slab, ((0, 0), (0, P_SIZE), (0, P_SIZE)))
    tile_rows = (jnp.arange(N_NARROW).astype(jnp.int32) * TR)[:, None, None]
    tile_cols = (jnp.arange(N_WIDE).astype(jnp.int32) * TC)[None, :, None]
    rows = (row_offset + tile_rows + jnp.zeros_like(row_offset)).reshape(-1).astype(jnp.int32)
    cols = (col_offset + tile_cols + jnp.zeros_like(col_offset)).reshape(-1).astype(jnp.int32)
    amps = amplitude.reshape(-1, P_SIZE, P_SIZE)
    lives = occupied.reshape(-1)
    zero = jnp.zeros((), jnp.int32)
    canvas = jnp.zeros((2, NR + P_SIZE, NC + P_SIZE), jnp.float32)
    probe_sum = jnp.zeros((2, P_SIZE, P_SIZE), jnp.float32)

    def visit(carry, item):
        grid, total = carry
        row_start, col_start, amp_block, live = item
        patch = lax.dynamic_slice(padded, (zero, row_start, col_start), (2, P_SIZE, P_SIZE))
        obj_term, probe_term = position_terms(patch, probe_wave, amp_block, live.astype(jnp.float32), tables)
        current = lax.dynamic_slice(grid, (zero, row_start, col_start), (2, P_SIZE, P_SIZE))
        grid = lax.dynamic_update_slice(grid, current + obj_term, (zero, row_start, col_start))
        return ((grid, total + probe_term), None)
    (canvas, probe_sum), unused = lax.scan(visit, (canvas, probe_sum), (rows, cols, amps, lives))
    object_grad = canvas[:, :NR, :NC].astype(jnp.bfloat16)
    probe_grad = probe_sum * (1.0 / math.sqrt(N_NARROW * N_WIDE * N_PROBE))
    return (object_grad, probe_grad)
```

```python
import math

import jax
import jax.numpy as jnp
import numpy as np
from jax import lax
from jax.sharding import PartitionSpec as P


def from_behind(x, axis, by):
    length = lax.axis_size(axis)
    pairs = [(i, i + by) for i in range(length) if 0 <= i + by < length]
    return lax.ppermute(x, axis, pairs)


def swap(x):
    return lax.ppermute(x, "probe", [(0, 1), (1, 0)])


def dft_tables(size, period, rows):
    index = np.arange(size)
    product = ((np.arange(rows) % period)[:, None] * index[None, :]) % size
    angle = product.astype(np.float32) * np.float32(2.0 * math.pi / size)
    norm = np.float32(1.0 / math.sqrt(size))
    return (
        jnp.asarray(np.cos(angle) * norm, jnp.bfloat16),
        jnp.asarray(-np.sin(angle) * norm, jnp.bfloat16),
    )


def cyclic_tables(size, period, shift):
    cos_part, sin_part = dft_tables(size, period, 2 * period)
    zero = jnp.zeros((), jnp.int32)
    cos_part = lax.dynamic_slice(cos_part, (period - shift, zero), (period, size))
    sin_part = lax.dynamic_slice(sin_part, (period - shift, zero), (period, size))
    return jnp.concatenate(
        [jnp.concatenate([cos_part, sin_part], 1), jnp.concatenate([-sin_part, cos_part], 1)], 0
    )


def scatter_sum(x, axis, dim):
    length = lax.axis_size(axis)
    block = x.shape[dim] // length
    me = lax.axis_index(axis)

    def part(of):
        return lax.dynamic_slice_in_dim(x, of * block, block, dim)

    if length > 8:
        return lax.psum_scatter(x, axis, scatter_dimension=dim, tiled=True).astype(jnp.float32)
    total = part(me).astype(jnp.float32)
    for step in range(1, length):
        pairs = [(i, (i + step) % length) for i in range(length)]
        got = lax.ppermute(part(lax.rem(me + step, length)), axis, pairs)
        total = total + got.astype(jnp.float32)
    return total


def shards(object_slab, probe_wave, amplitude, row_offset, col_offset, occupied):
    bf16, f32 = jnp.bfloat16, jnp.float32
    size = probe_wave.shape[1]
    tile_rows, tile_cols = object_slab.shape[1:]
    core = lax.axis_index("probe")
    zero = jnp.zeros((), jnp.int32)
    row_start = row_offset[0, 0, 0]
    col_start = col_offset[0, 0, 0]
    corner = jnp.stack([row_start, col_start])
    other_corner = swap(corner)

    def ordered(mine, other):
        return jnp.where(core == 0, jnp.stack([mine, other]), jnp.stack([other, mine]))

    cut = size // 2
    plane = lax.dynamic_index_in_dim(object_slab, core, 0, keepdims=False)
    below_b = from_behind(plane[cut:size], "narrow", -1)
    right_a = from_behind(plane[:cut], "wide", -1)
    below_a = from_behind(plane[:cut], "narrow", -1)
    right_b = from_behind(plane[cut:], "wide", -1)
    diag_b = from_behind(below_b, "wide", -1)
    diag_a = from_behind(right_a, "narrow", -1)

    def both(*parts):
        return ordered(jnp.concatenate(parts, 0), jnp.concatenate([swap(p) for p in parts], 0))

    below = both(below_a, below_b)
    right = both(right_a, right_b)
    diag = both(diag_a, diag_b)

    right_side = cyclic_tables(size, tile_cols, col_start)
    left_inv = cyclic_tables(size, tile_rows, row_start)
    inv_right = right_side.T
    left_side = left_inv.T
    padded = jnp.pad(probe_wave, ((0, 0), (0, tile_rows - size), (0, 0)))
    padded = jnp.concatenate([padded, padded], 1)
    padded = jnp.concatenate([padded, padded], 2)
    probe = lax.dynamic_slice(
        padded, (zero, tile_rows - row_start, tile_cols - col_start), (2, tile_rows, tile_cols)
    ).astype(f32)
    row_at = lax.broadcasted_iota(jnp.int32, (tile_rows, tile_cols), 0)
    col_at = lax.broadcasted_iota(jnp.int32, (tile_rows, tile_cols), 1)

    grow = ((0, 0), (0, tile_rows - size), (0, 0))
    in_rows = row_at >= row_start
    in_cols = col_at >= col_start
    patch = jnp.where(
        in_rows,
        jnp.where(in_cols, object_slab, right),
        jnp.where(in_cols, jnp.pad(below, grow), jnp.pad(diag, grow)),
    ).astype(f32)

    exit_wave = jnp.concatenate(
        [
            (probe[0] * patch[0] - probe[1] * patch[1]).astype(bf16),
            (probe[0] * patch[1] + probe[1] * patch[0]).astype(bf16),
        ],
        1,
    )
    half = jnp.dot(exit_wave, right_side, preferred_element_type=f32).astype(bf16)
    half = jnp.concatenate([half[:, :size], half[:, size:]], 0)
    far = jnp.dot(left_side, half, preferred_element_type=f32)
    far_re, far_im = far[:size], far[size:]
    magnitude = jnp.sqrt(far_re * far_re + far_im * far_im)
    live = occupied[0, 0, 0].astype(f32)
    factor = (1.0 - amplitude[0, 0, 0].astype(f32) / jnp.maximum(magnitude, 1.0)) * live
    chi = jnp.concatenate([(far_re * factor).astype(bf16), (far_im * factor).astype(bf16)], 1)
    back_half = jnp.dot(chi, inv_right, preferred_element_type=f32).astype(bf16)
    back_half = jnp.concatenate([back_half[:, :tile_cols], back_half[:, tile_cols:]], 0)
    back = jnp.dot(left_inv, back_half, preferred_element_type=f32)
    back_re, back_im = back[:tile_rows], back[tile_rows:]
    obj = jnp.stack(
        [probe[0] * back_re + probe[1] * back_im, probe[0] * back_im - probe[1] * back_re]
    ).astype(bf16)
    probe_term = jnp.stack(
        [patch[0] * back_re + patch[1] * back_im, patch[0] * back_im - patch[1] * back_re]
    ).astype(bf16)

    sent = lax.dynamic_index_in_dim(obj, 1 - core, 0, keepdims=False)
    kept = lax.dynamic_index_in_dim(obj, core, 0, keepdims=False).astype(f32)
    got = swap(sent).astype(f32)
    got_rows = row_at >= other_corner[0]
    got_cols = col_at >= other_corner[1]

    def piece(rows_in, cols_in):
        mine = (in_rows == rows_in) & (in_cols == cols_in)
        theirs = (got_rows == rows_in) & (got_cols == cols_in)
        return jnp.where(mine, kept, 0.0) + jnp.where(theirs, got, 0.0)

    own = piece(True, True)
    to_right = piece(True, False)
    to_below = piece(False, True)[:size]
    to_diag = piece(False, False)[:size]
    from_diag_a = from_behind(to_diag[:cut].astype(bf16), "narrow", 1)
    from_diag_b = from_behind(to_diag[cut:].astype(bf16), "wide", 1)
    from_above_a = from_behind(to_below[:cut].astype(bf16), "narrow", 1)
    from_left_b = from_behind(to_right[cut:].astype(bf16), "wide", 1)
    from_left_a = from_behind((to_right[:cut] + from_diag_a.astype(f32)).astype(bf16), "wide", 1)
    from_above_b = from_behind((to_below[cut:] + from_diag_b.astype(f32)).astype(bf16), "narrow", 1)
    from_left = jnp.concatenate([from_left_a, from_left_b], 0).astype(f32)
    from_above = jnp.concatenate([from_above_a, from_above_b], 0).astype(f32)
    from_above = jnp.pad(from_above, ((0, tile_rows - size), (0, 0)))
    own = (own + from_left + from_above).astype(bf16)
    object_grad = ordered(own, swap(own))

    probe_term = jnp.concatenate([probe_term, probe_term], 1)
    probe_term = lax.dynamic_slice_in_dim(probe_term, row_start, size, 1)
    probe_term = jnp.concatenate([probe_term, probe_term], 2)
    probe_term = lax.dynamic_slice_in_dim(probe_term, col_start, size, 2)
    narrow, cores = lax.axis_size("narrow"), lax.axis_size("probe")
    width = size // (narrow * cores)
    by_core = probe_term.reshape(2, size, narrow, cores, width)
    sent = lax.dynamic_index_in_dim(by_core, 1 - core, 3, keepdims=False)
    kept = lax.dynamic_index_in_dim(by_core, core, 3, keepdims=False)
    total = kept.astype(f32) + swap(sent).astype(f32)
    total = total.astype(bf16).reshape(2, size, narrow * width)
    total = scatter_sum(total, "narrow", 2).astype(bf16)
    total = scatter_sum(total, "wide", 1)
    scale = 1.0 / math.sqrt(lax.axis_size("wide") * narrow * cores)
    return (object_grad, total * scale)


def solution(mesh):
    in_specs = (
        P(None, ("groups", "narrow"), "wide"),
        P(),
        P(("groups", "narrow"), "wide", "probe", None, None),
        P(("groups", "narrow"), "wide", "probe"),
        P(("groups", "narrow"), "wide", "probe"),
        P(("groups", "narrow"), "wide", "probe"),
    )
    out_specs = (
        P(None, ("groups", "narrow"), "wide"),
        P(None, ("groups", "wide"), ("narrow", "probe")),
    )
    return jax.shard_map(shards, mesh=mesh, in_specs=in_specs, out_specs=out_specs, check_vma=False)
```

```python
import functools
import math

import jax
import jax.numpy as jnp
import numpy as np
from jax import lax
from jax.experimental import pallas as pl
from jax.experimental.pallas import tpu as pltpu
from jax.sharding import PartitionSpec as P

BF16 = jnp.bfloat16
F32 = jnp.float32
VMEM = pl.BlockSpec(memory_space=pltpu.VMEM)
SMEM = pl.BlockSpec(memory_space=pltpu.SMEM)


def to_neighbour(x, by, along_narrow):
    wide, narrow, cores = (lax.axis_size(name) for name in ("wide", "narrow", "probe"))
    pairs = []
    for w in range(wide):
        for n in range(narrow):
            for core in range(cores):
                w_to, n_to = (w, n + by) if core == along_narrow else (w + by, n)
                if 0 <= w_to < wide and 0 <= n_to < narrow:
                    source = (w * narrow + n) * cores + core
                    pairs.append((source, (w_to * narrow + n_to) * cores + core))
    return lax.ppermute(x, ("wide", "narrow", "probe"), pairs)


def swap(x):
    return lax.ppermute(x, "probe", [(0, 1), (1, 0)])


def dft_tables(size):
    index = np.arange(size)
    product = (index[:, None] * index[None, :]) % size
    angle = product.astype(np.float32) * np.float32(2.0 * math.pi / size)
    norm = np.float32(1.0 / math.sqrt(size))
    return (
        jnp.asarray(np.cos(angle) * norm, BF16),
        jnp.asarray(-np.sin(angle) * norm, BF16),
    )


def dot(a, b):
    return jnp.dot(a, b, preferred_element_type=F32)


def iota(shape, dim):
    return lax.broadcasted_iota(jnp.int32, shape, dim)


def one_hot(equal):
    return jnp.where(equal, 1.0, 0.0).astype(BF16)


def cyclic(at, shift, period):
    back = at - shift
    return jnp.where(back < 0, back + period, back)


def call(kernel, out_shape, in_specs, scratch=(), flops=0, bytes_accessed=0, name=None):
    return pl.pallas_call(
        kernel,
        out_shape=out_shape,
        in_specs=in_specs,
        out_specs=jax.tree.map(lambda _: VMEM, out_shape),
        scratch_shapes=list(scratch),
        compiler_params=pltpu.CompilerParams(vmem_limit_bytes=48 * 1024 * 1024),
        cost_estimate=pl.CostEstimate(
            flops=flops, bytes_accessed=bytes_accessed, transcendentals=0
        ),
        name=name,
    )


def shift_tables(corner, cos_in, sin_in, probe_in, right, right_t, left_t, left, probe):
    size = cos_in.shape[0]
    rows, cols = probe.shape[1:]
    row_start, col_start = corner[0], corner[1]
    row_hot = one_hot(cyclic(iota((rows, size), 0), row_start, rows) == iota((rows, size), 1))
    row_hot_t = one_hot(cyclic(iota((size, rows), 1), row_start, rows) == iota((size, rows), 0))
    col_hot = one_hot(cyclic(iota((cols, size), 0), col_start, cols) == iota((cols, size), 1))
    col_hot_t = one_hot(cyclic(iota((size, cols), 1), col_start, cols) == iota((size, cols), 0))

    cos_part = dot(col_hot, cos_in[...]).astype(BF16)
    right[:cols, :size] = cos_part
    right[cols:, size:] = cos_part
    sin_part = dot(col_hot, sin_in[...])
    right[:cols, size:] = sin_part.astype(BF16)
    right[cols:, :size] = (-sin_part).astype(BF16)

    cos_part = dot(cos_in[...], col_hot_t).astype(BF16)
    right_t[:size, :cols] = cos_part
    right_t[size:, cols:] = cos_part
    sin_part = dot(sin_in[...], col_hot_t)
    right_t[size:, :cols] = sin_part.astype(BF16)
    right_t[:size, cols:] = (-sin_part).astype(BF16)

    cos_part = dot(row_hot, cos_in[...]).astype(BF16)
    left_t[:rows, :size] = cos_part
    left_t[rows:, size:] = cos_part
    sin_part = dot(row_hot, sin_in[...])
    left_t[:rows, size:] = sin_part.astype(BF16)
    left_t[rows:, :size] = (-sin_part).astype(BF16)

    cos_part = dot(cos_in[...], row_hot_t).astype(BF16)
    left[:size, :rows] = cos_part
    left[size:, rows:] = cos_part
    sin_part = dot(sin_in[...], row_hot_t)
    left[size:, :rows] = sin_part.astype(BF16)
    left[:size, rows:] = (-sin_part).astype(BF16)

    for plane in range(2):
        moved = dot(row_hot, probe_in[plane]).astype(BF16)
        probe[plane] = dot(moved, col_hot_t).astype(BF16)


def slot_terms(
    scalars, own, first, first2, second, second2, third, third2,
    right, right_t, left_t, left, probe, amplitude,
    sent, kept, term, exit_wave, half, chi, back_half, patch, obj,
):
    rows, cols = own.shape[1:]
    size = chi.shape[0]
    cut = first.shape[1]
    row_start, col_start, core = scalars[0], scalars[1], scalars[2]
    live = scalars[3].astype(F32)
    step = 128
    in_cols = iota((step, cols), 1) >= col_start
    core_0 = iota((step, cols), 0) * 0 + core == 0
    for start in range(0, rows, step):
        at = pl.ds(start, step)
        in_rows = iota((step, cols), 0) + start >= row_start
        upper = start < cut
        sub = pl.ds(start if upper else start - cut, step)
        planes = []
        for plane in range(2):

            def load(on_core_0, on_core_1):
                a, b = on_core_0[plane, sub], on_core_1[plane, sub]
                return jnp.where(core_0, a.astype(F32), b.astype(F32))

            side = load(first2, first) if upper else load(second2, second)
            value = jnp.where(in_cols, own[plane, at].astype(F32), side)
            if start < size:
                below = load(second, second2) if upper else load(first, first2)
                diag = load(third2, third) if upper else load(third, third2)
                value = jnp.where(in_rows, value, jnp.where(in_cols, below, diag))
            patch[plane, at] = value.astype(BF16)
            planes.append(value)
        probe_re, probe_im = probe[0, at].astype(F32), probe[1, at].astype(F32)
        exit_wave[at, :cols] = (probe_re * planes[0] - probe_im * planes[1]).astype(BF16)
        exit_wave[at, cols:] = (probe_re * planes[1] + probe_im * planes[0]).astype(BF16)

    half[:rows] = dot(exit_wave[...], right[:, :size]).astype(BF16)
    half[rows:] = dot(exit_wave[...], right[:, size:]).astype(BF16)
    wide = 256
    for start in range(0, size, wide):
        far = dot(left[...], half[:, start : start + wide])
        far_re, far_im = far[:size], far[size:]
        magnitude = jnp.sqrt(far_re * far_re + far_im * far_im)
        amp = amplitude[:, start : start + wide].astype(F32)
        factor = (1.0 - amp / jnp.maximum(magnitude, 1.0)) * live
        chi[:, start : start + wide] = (far_re * factor).astype(BF16)
        chi[:, size + start : size + start + wide] = (far_im * factor).astype(BF16)
    back_half[:size] = dot(chi[...], right_t[:, :cols]).astype(BF16)
    back_half[size:] = dot(chi[...], right_t[:, cols:]).astype(BF16)
    for start in range(0, cols, wide):
        at = slice(start, start + wide)
        back = dot(left_t[...], back_half[:, at])
        back_re, back_im = back[:rows], back[rows:]
        probe_re, probe_im = probe[0, :, at].astype(F32), probe[1, :, at].astype(F32)
        obj[0, :, at] = (probe_re * back_re + probe_im * back_im).astype(BF16)
        obj[1, :, at] = (probe_re * back_im - probe_im * back_re).astype(BF16)
        patch_re, patch_im = patch[0, :, at].astype(F32), patch[1, :, at].astype(F32)
        term[0, :, at] = (patch_re * back_re + patch_im * back_im).astype(BF16)
        term[1, :, at] = (patch_re * back_im - patch_im * back_re).astype(BF16)
    count = kept.shape[1]
    for plane in range(2):
        kept[plane] = obj[plane, pl.ds(pl.multiple_of(cut * core, 128), count)]
        sent[plane] = obj[plane, pl.ds(pl.multiple_of(cut * (1 - core), 128), count)]


def part_of(scalars, kept, got, base, at, rows_in, cols_in):
    shape = (at.size, kept.shape[2])
    row_at, col_at = iota(shape, 0) + (base + at.start), iota(shape, 1)
    masks = []
    for row_start, col_start in ((scalars[0], scalars[1]), (scalars[4], scalars[5])):
        in_rows = jnp.where(row_at >= row_start, 1, 0) == rows_in
        in_cols = jnp.where(col_at >= col_start, 1, 0) == cols_in
        masks.append(in_rows & in_cols)
    return [
        jnp.where(masks[0], kept[plane, at].astype(F32), 0.0)
        + jnp.where(masks[1], got[plane, at].astype(F32), 0.0)
        for plane in range(2)
    ]


def fill(scalars, kept, got, out, cut, rows_in, cols_in):
    step = 128
    for start in range(0, out.shape[1], step):
        at = pl.ds(start, step)
        part = part_of(scalars, kept, got, scalars[2] * cut, at, rows_in, cols_in)
        for plane in range(2):
            out[plane, at] = part[plane].astype(out.dtype)


def diag_part(scalars, kept, got, diag):
    fill(scalars, kept, got, diag, diag.shape[1], 0, 0)


def side_parts(scalars, kept, got, now, later, own):
    core, cut = scalars[2], later.shape[1]
    fill(scalars, kept, got, now, cut, core, 1 - core)
    fill(scalars, kept, got, later, cut, 1 - core, core)
    fill(scalars, kept, got, own, cut, 1, 1)


def add_kernel(a, b, out):
    out[...] = (a[...].astype(F32) + b[...].astype(F32)).astype(out.dtype)


def total_kernel(own, a, b, out):
    cut = b.shape[1]
    for plane in range(2):
        total = own[plane, :cut] + a[plane, :cut].astype(F32) + b[plane].astype(F32)
        out[plane, :cut] = total.astype(BF16)
        out[plane, cut:] = (own[plane, cut:] + a[plane, cut:].astype(F32)).astype(BF16)


def probe_parts(scalars, term, sent, kept):
    rows, cols = term.shape[1:]
    narrow, wide, _, height, width = sent.shape
    size = wide * height
    row_start, col_start, core = scalars[0], scalars[1], scalars[2]
    row_hot = one_hot(cyclic(iota((size, rows), 1), row_start, rows) == iota((size, rows), 0))
    for plane in range(2):
        moved = dot(row_hot, term[plane]).astype(BF16)
        for block in range(narrow):
            for out, owner in ((kept, core), (sent, 1 - core)):
                column = iota((cols, width), 1) + (block * 2 + owner) * width
                hot = one_hot(cyclic(iota((cols, width), 0), col_start, cols) == column)
                result = dot(moved, hot).astype(BF16)
                for row in range(wide):
                    out[block, row, plane] = result[row * height : (row + 1) * height]


def scatter_sum(x, axis):
    length = lax.axis_size(axis)
    if length > 8:
        total = lax.psum_scatter(x, axis, scatter_dimension=0, tiled=True)
        return total[0].astype(F32)
    me = lax.axis_index(axis)

    def part(of):
        return lax.dynamic_index_in_dim(x, of, 0, keepdims=False)

    total = part(me).astype(F32)
    for step in range(1, length):
        pairs = [(i, (i + step) % length) for i in range(length)]
        got = lax.ppermute(part(lax.rem(me + step, length)), axis, pairs)
        total = total + got.astype(F32)
    return total


def shards(object_slab, probe_wave, amplitude, row_offset, col_offset, occupied):
    size = probe_wave.shape[1]
    rows, cols = object_slab.shape[1:]
    core = lax.axis_index("probe")
    narrow, wide, cores = (lax.axis_size(name) for name in ("narrow", "wide", "probe"))
    corner = jnp.stack([row_offset[0, 0, 0], col_offset[0, 0, 0]])
    scalars = jnp.concatenate([corner, jnp.stack([core.astype(jnp.int32), occupied[0, 0, 0]])])

    def shape(*dims, dtype=BF16):
        return jax.ShapeDtypeStruct(dims, dtype)

    cut = size // 2
    count = rows - cut
    first = to_neighbour(lax.dynamic_slice_in_dim(object_slab, cut * (1 - core), cut, 1), -1, 0)
    second = to_neighbour(lax.dynamic_slice_in_dim(object_slab, cut * core, count, 1), -1, 0)
    third = to_neighbour(first, -1, 1)
    late_corner, first_late = lax.optimization_barrier((corner, first))

    cos_part, sin_part = dft_tables(size)
    tables = call(
        shift_tables,
        (
            shape(2 * cols, 2 * size),
            shape(2 * size, 2 * cols),
            shape(2 * rows, 2 * size),
            shape(2 * size, 2 * rows),
            shape(2, rows, cols),
        ),
        [SMEM] + [VMEM] * 3,
        flops=4 * 10**9,
        bytes_accessed=2 * 10**7,
        name="shift_tables",
    )(late_corner, cos_part, sin_part, probe_wave)
    second, tables = lax.optimization_barrier((second, tables))
    pieces = (first, swap(first_late), second, swap(second), third, swap(third))
    sent, kept, term = call(
        slot_terms,
        (shape(2, count, cols), shape(2, count, cols), shape(2, rows, cols)),
        [SMEM] + [VMEM] * 13,
        scratch=[
            pltpu.VMEM((rows, 2 * cols), BF16),
            pltpu.VMEM((2 * rows, size), BF16),
            pltpu.VMEM((size, 2 * size), BF16),
            pltpu.VMEM((2 * size, cols), BF16),
            pltpu.VMEM((2, rows, cols), BF16),
            pltpu.VMEM((2, rows, cols), BF16),
        ],
        flops=5 * 10**9,
        bytes_accessed=2 * 10**7,
        name="slot_terms",
    )(scalars, object_slab, *pieces, *tables, amplitude[0, 0, 0])

    got = swap(sent)
    scalars = jnp.concatenate([scalars, swap(corner)])
    diag = call(diag_part, shape(2, cut, cols), [SMEM, VMEM, VMEM], name="diag_part")(
        scalars, kept, got
    )
    from_first = to_neighbour(diag, 1, 0)
    now, later, own = call(
        side_parts,
        (
            shape(2, count, cols),
            shape(2, cut, cols, dtype=F32),
            shape(2, count, cols, dtype=F32),
        ),
        [SMEM, VMEM, VMEM],
        name="side_parts",
    )(scalars, kept, got)
    from_second = to_neighbour(now, 1, 0)
    later = call(add_kernel, shape(2, cut, cols), [VMEM, VMEM], name="add")(later, from_first)
    from_third = to_neighbour(later, 1, 1)
    own = call(total_kernel, shape(2, count, cols), [VMEM] * 3, name="total")(
        own, from_second, from_third
    )
    other = swap(own)
    object_grad = jnp.where(
        core == 0,
        jnp.concatenate([own[:, :cut], other], 1),
        jnp.concatenate([other[:, :cut], own], 1),
    )

    blocks = shape(narrow, wide, 2, size // wide, size // (narrow * cores))
    sent, kept = call(
        probe_parts,
        (blocks, blocks),
        [SMEM, VMEM],
        flops=2 * 10**9,
        name="probe_parts",
    )(scalars, term)
    total = (kept.astype(F32) + swap(sent).astype(F32)).astype(BF16)
    total = scatter_sum(total, "narrow").astype(BF16)
    total = scatter_sum(total, "wide")
    return (object_grad, total * (1.0 / math.sqrt(wide * narrow * cores)))


def solution(mesh):
    in_specs = (
        P(None, ("groups", "narrow"), "wide"),
        P(),
        P(("groups", "narrow"), "wide", "probe", None, None),
        P(("groups", "narrow"), "wide", "probe"),
        P(("groups", "narrow"), "wide", "probe"),
        P(("groups", "narrow"), "wide", "probe"),
    )
    out_specs = (
        P(None, ("groups", "narrow"), "wide"),
        P(None, ("groups", "wide"), ("narrow", "probe")),
    )
    return jax.shard_map(shards, mesh=mesh, in_specs=in_specs, out_specs=out_specs, check_vma=False)
```

```python
import functools
import math

import jax
import jax.numpy as jnp
import numpy as np
from jax import lax
from jax.experimental import pallas as pl
from jax.experimental.pallas import tpu as pltpu
from jax.sharding import PartitionSpec as P

BF16 = jnp.bfloat16
F32 = jnp.float32
VMEM = pl.BlockSpec(memory_space=pltpu.VMEM)
SMEM = pl.BlockSpec(memory_space=pltpu.SMEM)
ANY = pl.BlockSpec(memory_space=pl.ANY)


def to_neighbour(x, by, along_narrow, senders=(0, 1)):
    wide, narrow, cores = (lax.axis_size(name) for name in ("wide", "narrow", "probe"))
    pairs = []
    for w in range(wide):
        for n in range(narrow):
            for core in senders:
                w_to, n_to = (w, n + by) if core == along_narrow else (w + by, n)
                if 0 <= w_to < wide and 0 <= n_to < narrow:
                    source = (w * narrow + n) * cores + core
                    pairs.append((source, (w_to * narrow + n_to) * cores + core))
    return lax.ppermute(x, ("wide", "narrow", "probe"), pairs)


def swap(x):
    return lax.ppermute(x, "probe", [(0, 1), (1, 0)])


def dft_tables(size):
    index = np.arange(size)
    product = (index[:, None] * index[None, :]) % size
    angle = product.astype(np.float32) * np.float32(2.0 * math.pi / size)
    norm = np.float32(1.0 / math.sqrt(size))
    return (
        jnp.asarray(np.cos(angle) * norm, BF16),
        jnp.asarray(-np.sin(angle) * norm, BF16),
    )


def dot(a, b):
    return jnp.dot(a, b, preferred_element_type=F32)


def iota(shape, dim):
    return lax.broadcasted_iota(jnp.int32, shape, dim)


def one_hot(equal):
    return jnp.where(equal, 1.0, 0.0).astype(BF16)


def cyclic(at, shift, period):
    back = at - shift
    return jnp.where(back < 0, back + period, back)


def call(kernel, out_shape, in_specs, vmem, scratch=(), flops=0, bytes_accessed=0, name=None):
    return pl.pallas_call(
        kernel,
        out_shape=out_shape,
        in_specs=in_specs,
        out_specs=jax.tree.map(lambda _: VMEM, out_shape),
        scratch_shapes=list(scratch),
        compiler_params=pltpu.CompilerParams(vmem_limit_bytes=vmem * 1024 * 1024),
        cost_estimate=pl.CostEstimate(
            flops=flops, bytes_accessed=bytes_accessed, transcendentals=0
        ),
        name=name,
    )


def shift_tables(
    width, scalars, cos_in, sin_in, probe_in,
    right, right_t, left_t, left, probe, back_rows, back_cols, back_cols2,
):
    size = cos_in.shape[0]
    rows, cols = probe.shape[1:]
    row_start, col_start, core = scalars[0], scalars[1], scalars[2]
    row_hot = one_hot(cyclic(iota((rows, size), 0), row_start, rows) == iota((rows, size), 1))
    row_hot_t = one_hot(cyclic(iota((size, rows), 1), row_start, rows) == iota((size, rows), 0))
    col_hot = one_hot(cyclic(iota((cols, size), 0), col_start, cols) == iota((cols, size), 1))
    col_hot_t = one_hot(cyclic(iota((size, cols), 1), col_start, cols) == iota((size, cols), 0))

    back_rows[...] = row_hot_t
    count = back_cols.shape[1]
    for out, owner in ((back_cols, core), (back_cols2, 1 - core)):
        at = iota((cols, count), 1)
        column = at + (at // width + owner) * width
        out[...] = one_hot(cyclic(iota((cols, count), 0), col_start, cols) == column)

    cos_part = dot(col_hot, cos_in[...]).astype(BF16)
    right[:cols, :size] = cos_part
    right[cols:, size:] = cos_part
    sin_part = dot(col_hot, sin_in[...])
    right[:cols, size:] = sin_part.astype(BF16)
    right[cols:, :size] = (-sin_part).astype(BF16)

    cos_part = dot(cos_in[...], col_hot_t).astype(BF16)
    right_t[:size, :cols] = cos_part
    right_t[size:, cols:] = cos_part
    sin_part = dot(sin_in[...], col_hot_t)
    right_t[size:, :cols] = sin_part.astype(BF16)
    right_t[:size, cols:] = (-sin_part).astype(BF16)

    cos_part = dot(row_hot, cos_in[...]).astype(BF16)
    left_t[:rows, :size] = cos_part
    left_t[rows:, size:] = cos_part
    sin_part = dot(row_hot, sin_in[...])
    left_t[:rows, size:] = sin_part.astype(BF16)
    left_t[rows:, :size] = (-sin_part).astype(BF16)

    cos_part = dot(cos_in[...], row_hot_t).astype(BF16)
    left[:size, :rows] = cos_part
    left[size:, rows:] = cos_part
    sin_part = dot(sin_in[...], row_hot_t)
    left[size:, :rows] = sin_part.astype(BF16)
    left[:size, rows:] = (-sin_part).astype(BF16)

    for plane in range(2):
        moved = dot(row_hot, probe_in[plane]).astype(BF16)
        probe[plane] = dot(moved, col_hot_t).astype(BF16)


def slot_terms(
    scalars, own, first, first2, second, second2, third, third2,
    right, right_t, left_t, left, probe, back_rows, back_cols, back_cols2, amplitude,
    sent, kept, probe_sent, probe_kept, exit_wave, half, chi, back_half, patch, obj, term,
):
    rows, cols = own.shape[1:]
    size = chi.shape[0]
    cut = first.shape[1]
    row_start, col_start, core = scalars[0], scalars[1], scalars[2]
    live = scalars[3].astype(F32)
    step = 128
    in_cols = iota((step, cols), 1) >= col_start
    core_0 = iota((step, cols), 0) * 0 + core == 0
    for start in range(0, rows, step):
        at = pl.ds(start, step)
        in_rows = iota((step, cols), 0) + start >= row_start
        upper = start < cut
        sub = pl.ds(start if upper else start - cut, step)
        planes = []
        for plane in range(2):

            def load(on_core_0, on_core_1):
                a, b = on_core_0[plane, sub], on_core_1[plane, sub]
                return jnp.where(core_0, a.astype(F32), b.astype(F32))

            side = load(first2, first) if upper else load(second2, second)
            value = jnp.where(in_cols, own[plane, at].astype(F32), side)
            if start < size:
                below = load(second, second2) if upper else load(first, first2)
                diag = load(third2, third) if upper else load(third, third2)
                value = jnp.where(in_rows, value, jnp.where(in_cols, below, diag))
            patch[plane, at] = value.astype(BF16)
            planes.append(value)
        probe_re, probe_im = probe[0, at].astype(F32), probe[1, at].astype(F32)
        exit_wave[at, :cols] = (probe_re * planes[0] - probe_im * planes[1]).astype(BF16)
        exit_wave[at, cols:] = (probe_re * planes[1] + probe_im * planes[0]).astype(BF16)

    half[:rows] = dot(exit_wave[...], right[:, :size]).astype(BF16)
    half[rows:] = dot(exit_wave[...], right[:, size:]).astype(BF16)
    wide = 256
    for start in range(0, size, wide):
        far = dot(left[...], half[:, start : start + wide])
        far_re, far_im = far[:size], far[size:]
        magnitude = jnp.sqrt(far_re * far_re + far_im * far_im)
        amp = amplitude[:, start : start + wide].astype(F32)
        factor = (1.0 - amp / jnp.maximum(magnitude, 1.0)) * live
        chi[:, start : start + wide] = (far_re * factor).astype(BF16)
        chi[:, size + start : size + start + wide] = (far_im * factor).astype(BF16)
    back_half[:size] = dot(chi[...], right_t[:, :cols]).astype(BF16)
    back_half[size:] = dot(chi[...], right_t[:, cols:]).astype(BF16)
    for start in range(0, cols, wide):
        at = slice(start, start + wide)
        back = dot(left_t[...], back_half[:, at])
        back_re, back_im = back[:rows], back[rows:]
        probe_re, probe_im = probe[0, :, at].astype(F32), probe[1, :, at].astype(F32)
        obj[0, :, at] = (probe_re * back_re + probe_im * back_im).astype(BF16)
        obj[1, :, at] = (probe_re * back_im - probe_im * back_re).astype(BF16)
        patch_re, patch_im = patch[0, :, at].astype(F32), patch[1, :, at].astype(F32)
        term[0, :, at] = (patch_re * back_re + patch_im * back_im).astype(BF16)
        term[1, :, at] = (patch_re * back_im - patch_im * back_re).astype(BF16)
    count = kept.shape[1]
    for plane in range(2):
        kept[plane] = obj[plane, pl.ds(pl.multiple_of(cut * core, 128), count)]
        sent[plane] = obj[plane, pl.ds(pl.multiple_of(cut * (1 - core), 128), count)]

    narrow, blocks, _, height, width = probe_sent.shape
    for plane in range(2):
        moved = dot(back_rows[...], term[plane]).astype(BF16)
        for out, hot in ((probe_sent, back_cols2), (probe_kept, back_cols)):
            result = dot(moved, hot[...]).astype(BF16)
            for column in range(narrow):
                for row in range(blocks):
                    out[column, row, plane] = result[
                        row * height : (row + 1) * height, column * width : (column + 1) * width
                    ]


def part_of(scalars, kept, got, cut, at, rows_in, cols_in):
    shape = (at.size, kept.shape[2])
    row_at, col_at = iota(shape, 0) + (scalars[2] * cut + at.start), iota(shape, 1)
    masks = []
    for row_start, col_start in ((scalars[0], scalars[1]), (scalars[5], scalars[6])):
        in_rows = jnp.where(row_at >= row_start, 1, 0) == rows_in
        in_cols = jnp.where(col_at >= col_start, 1, 0) == cols_in
        masks.append(in_rows & in_cols)
    return [
        jnp.where(masks[0], kept[plane, at].astype(F32), 0.0)
        + jnp.where(masks[1], got[plane, at].astype(F32), 0.0)
        for plane in range(2)
    ]


def tile_part(cut, rows_in, cols_in, scalars, kept, got, *refs):
    *arrived, out = refs
    fill(cut, 0, rows_in, cols_in, scalars, kept, got, arrived, out)


def fill(cut, first, rows_in, cols_in, scalars, kept, got, arrived, out):
    step = 128
    for start in range(0, out.shape[1], step):
        at = pl.ds(start, step)
        part = part_of(scalars, kept, got, cut, pl.ds(first + start, step), rows_in, cols_in)
        for plane in range(2):
            for more in arrived:
                part[plane] = part[plane] + more[plane, at].astype(F32)
            out[plane, at] = part[plane].astype(BF16)


def now_parts(cut, scalars, before, kept, got, upper, lower):
    core = scalars[2]
    fill(cut, 0, core, 1 - core, scalars, kept, got, (), upper)
    fill(cut, upper.shape[1], core, 1 - core, scalars, kept, got, (), lower)


def own_part(cut, scalars, before, kept, got, upper, lower, third, out):
    fill(cut, 0, 1, 1, scalars, kept, got, (upper, third), out.at[:, :cut])
    fill(cut, cut, 1, 1, scalars, kept, got, (lower,), out.at[:, cut:])


def probe_sum(narrow, scalars, diag, probe_kept, probe_got, *outs):
    me = scalars[4]
    for step, out in enumerate(outs):
        block = lax.rem(me + step, narrow)
        total = probe_kept[block].astype(F32) + probe_got[block].astype(F32)
        out[...] = total.astype(BF16)


def sum_kernel(*refs):
    *terms, out = refs
    total = terms[0][...].astype(F32)
    for term in terms[1:]:
        total = total + term[...].astype(F32)
    out[...] = total.astype(out.dtype)


def scaled_sum(scale, *refs):
    *terms, out = refs
    sum_kernel(*terms, out)
    out[...] = out[...] * scale


def sum_of(*terms):
    return call(
        sum_kernel,
        jax.ShapeDtypeStruct(terms[0].shape, BF16),
        [VMEM] * len(terms),
        8,
        flops=8 * 10**9,
        name="sum",
    )(*terms)


def scatter_parts(x, axis):
    length = lax.axis_size(axis)
    if length > 8:
        return [lax.psum_scatter(x, axis, scatter_dimension=0, tiled=True)[0]]
    me = lax.axis_index(axis)

    def part(of):
        return lax.dynamic_index_in_dim(x, of, 0, keepdims=False)

    terms = [part(me)]
    for step in range(1, length):
        if length & (length - 1):
            pairs = [(i, (i + step) % length) for i in range(length)]
            to = lax.rem(me + step, length)
        else:
            pairs = [(i, i ^ step) for i in range(length)]
            to = me ^ step
        terms.append(lax.ppermute(part(to), axis, pairs))
    return terms


def shards(object_slab, probe_wave, amplitude, row_offset, col_offset, occupied):
    size = probe_wave.shape[1]
    rows, cols = object_slab.shape[1:]
    core = lax.axis_index("probe")
    narrow, wide, cores = (lax.axis_size(name) for name in ("narrow", "wide", "probe"))
    corner = jnp.stack([row_offset[0, 0, 0], col_offset[0, 0, 0]])
    here = [core, occupied[0, 0, 0], lax.axis_index("narrow")]
    scalars = jnp.concatenate([corner, jnp.stack([x.astype(jnp.int32) for x in here])])

    def shape(*dims, dtype=BF16):
        return jax.ShapeDtypeStruct(dims, dtype)

    cut = size // 2
    count = rows - cut
    first = to_neighbour(lax.dynamic_slice_in_dim(object_slab, cut * (1 - core), cut, 1), -1, 0)
    second = to_neighbour(lax.dynamic_slice_in_dim(object_slab, cut * core, count, 1), -1, 0)
    third = to_neighbour(first, -1, 1)
    late_scalars, first_late = lax.optimization_barrier((scalars, first))

    cos_part, sin_part = dft_tables(size)
    width = size // (narrow * cores)
    tables = call(
        functools.partial(shift_tables, width),
        (
            shape(2 * cols, 2 * size),
            shape(2 * size, 2 * cols),
            shape(2 * rows, 2 * size),
            shape(2 * size, 2 * rows),
            shape(2, rows, cols),
            shape(size, rows),
            shape(cols, narrow * width),
            shape(cols, narrow * width),
        ),
        [SMEM] + [VMEM] * 3,
        20,
        flops=4 * 10**9,
        bytes_accessed=2 * 10**7,
        name="shift_tables",
    )(late_scalars, cos_part, sin_part, probe_wave)
    second, tables = lax.optimization_barrier((second, tables))
    pieces = (first, swap(first_late), second, swap(second), third, swap(third))
    blocks = shape(narrow, wide, 2, size // wide, width)
    sent, kept, probe_sent, probe_kept = call(
        slot_terms,
        (shape(2, count, cols), shape(2, count, cols), blocks, blocks),
        [SMEM] + [VMEM] * 16,
        18,
        scratch=[
            pltpu.VMEM((rows, 2 * cols), BF16),
            pltpu.VMEM((2 * rows, size), BF16),
            pltpu.VMEM((size, 2 * size), BF16),
            pltpu.VMEM((2 * size, cols), BF16),
            pltpu.VMEM((2, rows, cols), BF16),
            pltpu.VMEM((2, rows, cols), BF16),
            pltpu.VMEM((2, rows, cols), BF16),
        ],
        flops=6 * 10**9,
        bytes_accessed=2 * 10**7,
        name="slot_terms",
    )(scalars, object_slab, *pieces, *tables, amplitude[0, 0, 0])

    got, probe_got = swap(sent), swap(probe_sent)
    scalars = jnp.concatenate([scalars, swap(corner)])

    def tile(name, kernel, height, *more, after=()):
        return call(
            functools.partial(kernel, cut, len(after)),
            shape(2, height, cols),
            [SMEM] + [ANY] * len(after) + [VMEM] * (2 + len(more)),
            8,
            name=name,
        )(scalars, *after, kept, got, *more)

    def diag_part(cut, skip, scalars, *refs):
        tile_part(cut, 0, 0, scalars, *refs[skip:])

    def later_part(cut, skip, scalars, *refs):
        tile_part(cut, 1 - scalars[2], scalars[2], scalars, *refs[skip:])

    diag = tile("diag_part", diag_part, cut)
    from_first = to_neighbour(diag, 1, 0)
    probe_blocks = call(
        functools.partial(probe_sum, narrow),
        (jax.ShapeDtypeStruct(blocks.shape[1:], BF16),) * narrow,
        [SMEM, ANY, VMEM, VMEM],
        8,
        name="probe_sum",
    )(scalars, diag, probe_kept, probe_got)
    upper, lower = call(
        functools.partial(now_parts, cut),
        (shape(2, cut, cols), shape(2, count - cut, cols)),
        [SMEM, ANY, VMEM, VMEM],
        8,
        name="now_parts",
    )(scalars, probe_blocks[0], kept, got)
    from_upper = to_neighbour(upper, 1, 0)
    from_lower = to_neighbour(lower, 1, 0, senders=(1,))
    from_third = to_neighbour(tile("later_part", later_part, cut, from_first), 1, 1)
    received = [
        lax.ppermute(block, "narrow", [(i, (i + step) % narrow) for i in range(narrow)])
        for step, block in enumerate(probe_blocks)
        if step
    ]
    total = sum_of(probe_blocks[0], *received)
    terms = scatter_parts(total, "wide")
    probe_grad = call(
        functools.partial(scaled_sum, 1.0 / math.sqrt(wide * narrow * cores)),
        jax.ShapeDtypeStruct(terms[0].shape, F32),
        [VMEM] * len(terms),
        8,
        flops=20 * 10**9,
        name="probe_grad",
    )(*terms)
    own = call(
        functools.partial(own_part, cut),
        shape(2, count, cols),
        [SMEM, ANY] + [VMEM] * 5,
        8,
        flops=1 * 10**9,
        name="own_part",
    )(scalars, total, kept, got, from_upper, from_lower, from_third)
    other = swap(own)
    object_grad = jnp.where(
        core == 0,
        jnp.concatenate([own[:, :cut], other], 1),
        jnp.concatenate([other[:, :cut], own], 1),
    )
    return (object_grad, probe_grad)


def solution(mesh):
    in_specs = (
        P(None, ("groups", "narrow"), "wide"),
        P(),
        P(("groups", "narrow"), "wide", "probe", None, None),
        P(("groups", "narrow"), "wide", "probe"),
        P(("groups", "narrow"), "wide", "probe"),
        P(("groups", "narrow"), "wide", "probe"),
    )
    out_specs = (
        P(None, ("groups", "narrow"), "wide"),
        P(None, ("groups", "wide"), ("narrow", "probe")),
    )
    return jax.shard_map(shards, mesh=mesh, in_specs=in_specs, out_specs=out_specs, check_vma=False)
```

```python
import functools
import math

import jax
import jax.numpy as jnp
import numpy as np
from jax import lax
from jax.experimental import pallas as pl
from jax.experimental.pallas import tpu as pltpu
from jax.sharding import PartitionSpec as P

BF16 = jnp.bfloat16
F32 = jnp.float32
VMEM = pl.BlockSpec(memory_space=pltpu.VMEM)
SMEM = pl.BlockSpec(memory_space=pltpu.SMEM)
ANY = pl.BlockSpec(memory_space=pl.ANY)


def to_neighbour(x, by, along_narrow, senders=(0, 1)):
    wide, narrow, cores = (lax.axis_size(name) for name in ("wide", "narrow", "probe"))
    pairs = []
    for w in range(wide):
        for n in range(narrow):
            for core in senders:
                w_to, n_to = (w, n + by) if core == along_narrow else (w + by, n)
                if 0 <= w_to < wide and 0 <= n_to < narrow:
                    source = (w * narrow + n) * cores + core
                    pairs.append((source, (w_to * narrow + n_to) * cores + core))
    return lax.ppermute(x, ("wide", "narrow", "probe"), pairs)


def swap(x):
    return lax.ppermute(x, "probe", [(0, 1), (1, 0)])


def halves_first(size):
    return np.concatenate([np.arange(0, size, 2), np.arange(1, size, 2)])


def dft_tables(size):
    product = (np.arange(size)[:, None] * halves_first(size)[None, :]) % size
    angle = product.astype(np.float32) * np.float32(2.0 * math.pi / size)
    norm = np.float32(1.0 / math.sqrt(size))
    pair = (np.cos(angle) * norm, -np.sin(angle) * norm)
    return [jnp.asarray(x, BF16) for x in pair + tuple(x.T for x in pair)]


def dot(a, b):
    return jnp.dot(a, b, preferred_element_type=F32)


def iota(shape, dim):
    return lax.broadcasted_iota(jnp.int32, shape, dim)


def one_hot(equal):
    return jnp.where(equal, 1.0, 0.0).astype(BF16)


def cyclic(at, shift, period):
    back = at - shift
    return jnp.where(back < 0, back + period, back)


def call(kernel, out_shape, in_specs, vmem, scratch=(), flops=0, bytes_accessed=0, name=None):
    return pl.pallas_call(
        kernel,
        out_shape=out_shape,
        in_specs=in_specs,
        out_specs=jax.tree.map(lambda _: VMEM, out_shape),
        scratch_shapes=list(scratch),
        compiler_params=pltpu.CompilerParams(vmem_limit_bytes=vmem * 1024 * 1024),
        cost_estimate=pl.CostEstimate(
            flops=flops, bytes_accessed=bytes_accessed, transcendentals=0
        ),
        name=name,
    )


def shift_tables(
    width, scalars, cos_in, sin_in, cos_t, sin_t, probe_in, amp_in,
    right, right_t, left_t, left, probe, amplitude, back_rows, back_cols, back_cols2,
):
    size = cos_in.shape[0]
    part = size // 2
    row_start, col_start, core = scalars[0], scalars[1], scalars[2]
    row_start = jnp.where(row_start >= size, row_start - size, row_start)
    full = (size, size)

    back_rows[...] = one_hot(cyclic(iota(full, 1), row_start, size) == iota(full, 0))
    count = back_cols.shape[1]
    for out, owner in ((back_cols, core), (back_cols2, 1 - core)):
        at = iota((size, count), 1)
        column = at + (at // width + owner) * width
        out[...] = one_hot(cyclic(iota((size, count), 0), col_start, size) == column)

    for start, table, table_t in ((col_start, right, right_t), (row_start, left_t, left)):
        hot = one_hot(cyclic(iota((part, size), 0), start, size) == iota((part, size), 1))
        hot_t = one_hot(cyclic(iota((size, part), 1), start, size) == iota((size, part), 0))
        cos_part, sin_part = dot(hot, cos_in[...]), dot(hot, sin_in[...])
        cos_turn, sin_turn = dot(cos_t[...], hot_t), dot(sin_t[...], hot_t)
        for odd in range(2):
            at = slice(odd * part, (odd + 1) * part)
            table[odd, :part, :part] = cos_part[:, at].astype(BF16)
            table[odd, part:, part:] = cos_part[:, at].astype(BF16)
            table[odd, :part, part:] = sin_part[:, at].astype(BF16)
            table[odd, part:, :part] = (-sin_part[:, at]).astype(BF16)
            table_t[odd, :part, :part] = cos_turn[at].astype(BF16)
            table_t[odd, part:, part:] = cos_turn[at].astype(BF16)
            table_t[odd, part:, :part] = sin_turn[at].astype(BF16)
            table_t[odd, :part, part:] = (-sin_turn[at]).astype(BF16)

    row_hot = one_hot(cyclic(iota(full, 0), row_start, size) == iota(full, 1))
    col_hot_t = one_hot(cyclic(iota(full, 1), col_start, size) == iota(full, 0))
    for plane in range(2):
        moved = dot(row_hot, probe_in[plane]).astype(BF16)
        probe[plane] = dot(moved, col_hot_t).astype(BF16)

    def frequency(at):
        return jnp.where(at < part, 2 * at, 2 * at - (size - 1))

    moved = dot(one_hot(frequency(iota(full, 0)) == iota(full, 1)), amp_in[...]).astype(BF16)
    amplitude[...] = dot(moved, one_hot(frequency(iota(full, 1)) == iota(full, 0))).astype(BF16)


def slot_terms(
    scalars, own, first, first2, second, second2, third, third2,
    right, right_t, left_t, left, probe, amplitude, back_rows, back_cols, back_cols2,
    sent, kept, probe_sent, probe_kept, exit_wave, half, chi, back_half, patch, obj, term,
):
    rows, size = own.shape[1:]
    cut = first.shape[1]
    part = size // 2
    row_start, col_start, core = scalars[0], scalars[1], scalars[2]
    live = scalars[3].astype(F32)
    step = 128
    in_cols = iota((step, size), 1) >= col_start
    core_0 = iota((step, size), 0) * 0 + core == 0

    def tile_value(plane, row):
        def load(on_core_0, on_core_1, at):
            a, b = on_core_0[plane, pl.ds(at, step)], on_core_1[plane, pl.ds(at, step)]
            return jnp.where(core_0, a.astype(F32), b.astype(F32))

        if row < rows:
            here = own[plane, pl.ds(row, step)].astype(F32)
            side = load(first2, first, row) if row < cut else load(second2, second, row - cut)
        elif row - rows < cut:
            here = load(second, second2, row - rows)
            side = load(third2, third, row - rows)
        else:
            here = load(first, first2, row - rows - cut)
            side = load(third, third2, row - rows - cut)
        return jnp.where(in_cols, here, side)

    for start in range(0, size, step):
        at = pl.ds(start, step)
        planes = []
        for plane in range(2):
            row = start
            while row < rows:
                row += size
            value = tile_value(plane, row)
            while row > start:
                row -= size
                in_rows = iota((step, size), 0) + row >= row_start
                value = jnp.where(in_rows, tile_value(plane, row), value)
            patch[plane, at] = value.astype(BF16)
            planes.append(value)
        probe_re, probe_im = probe[0, at].astype(F32), probe[1, at].astype(F32)
        exit_re = probe_re * planes[0] - probe_im * planes[1]
        exit_im = probe_re * planes[1] + probe_im * planes[0]
        for plane, value in ((0, exit_re), (1, exit_im)):
            where = slice(plane * part, (plane + 1) * part)
            exit_wave[0, at, where] = (value[:, :part] + value[:, part:]).astype(BF16)
            exit_wave[1, at, where] = (value[:, :part] - value[:, part:]).astype(BF16)

    for odd in range(2):
        result = dot(exit_wave[odd], right[odd])
        cols = slice(odd * part, (odd + 1) * part)
        for plane in range(2):
            where = slice(plane * part, (plane + 1) * part)
            low, high = result[:part, where], result[part:, where]
            half[0, where, cols] = (low + high).astype(BF16)
            half[1, where, cols] = (low - high).astype(BF16)
    for odd in range(2):
        far = dot(left[odd], half[odd])
        far_re, far_im = far[:part], far[part:]
        magnitude = jnp.sqrt(far_re * far_re + far_im * far_im)
        at = slice(odd * part, (odd + 1) * part)
        factor = (1.0 - amplitude[at].astype(F32) / jnp.maximum(magnitude, 1.0)) * live
        for plane, value in ((0, far_re * factor), (1, far_im * factor)):
            where = slice(plane * part, (plane + 1) * part)
            chi[0, at, where] = value[:, :part].astype(BF16)
            chi[1, at, where] = value[:, part:].astype(BF16)
    for plane in range(2):
        where = slice(plane * part, (plane + 1) * part)
        even, odd = dot(chi[0], right_t[0, :, where]), dot(chi[1], right_t[1, :, where])
        for parity in range(2):
            at = slice(parity * part, (parity + 1) * part)
            back_half[parity, where, :part] = (even[at] + odd[at]).astype(BF16)
            back_half[parity, where, part:] = (even[at] - odd[at]).astype(BF16)
    for start in range(0, size, part):
        at = slice(start, start + part)
        even, odd = dot(left_t[0], back_half[0, :, at]), dot(left_t[1], back_half[1, :, at])
        for lines, back in ((slice(0, part), even + odd), (slice(part, size), even - odd)):
            back_re, back_im = back[:part], back[part:]
            probe_re, probe_im = probe[0, lines, at].astype(F32), probe[1, lines, at].astype(F32)
            obj[0, lines, at] = (probe_re * back_re + probe_im * back_im).astype(BF16)
            obj[1, lines, at] = (probe_re * back_im - probe_im * back_re).astype(BF16)
            patch_re, patch_im = patch[0, lines, at].astype(F32), patch[1, lines, at].astype(F32)
            term[0, lines, at] = (patch_re * back_re + patch_im * back_im).astype(BF16)
            term[1, lines, at] = (patch_re * back_im - patch_im * back_re).astype(BF16)
    count = kept.shape[1]
    for plane in range(2):
        obj[plane, size:] = obj[plane, : obj.shape[1] - size]
        kept[plane] = obj[plane, pl.ds(pl.multiple_of(cut * core, 128), count)]
        sent[plane] = obj[plane, pl.ds(pl.multiple_of(cut * (1 - core), 128), count)]

    narrow, blocks, _, height, width = probe_sent.shape
    for plane in range(2):
        moved = dot(back_rows[...], term[plane]).astype(BF16)
        for out, hot in ((probe_sent, back_cols2), (probe_kept, back_cols)):
            result = dot(moved, hot[...]).astype(BF16)
            for column in range(narrow):
                for row in range(blocks):
                    out[column, row, plane] = result[
                        row * height : (row + 1) * height, column * width : (column + 1) * width
                    ]


def part_of(scalars, kept, got, shape, cut, start, rows_in, cols_in):
    rows, size = shape
    step, cols = 128, kept.shape[2]
    below = (1 - rows_in) * (rows - size)
    at = pl.ds(start + below if isinstance(below, int) else pl.multiple_of(start + below, 128), step)
    row_at = iota((step, cols), 0) + (scalars[2] * cut + start + (1 - rows_in) * rows)
    col_at = iota((step, cols), 1)
    masks = []
    for row_start, col_start in ((scalars[0], scalars[1]), (scalars[5], scalars[6])):
        in_cols = jnp.where(col_at >= col_start, 1, 0) == cols_in
        masks.append((row_at >= row_start) & (row_at < row_start + size) & in_cols)
    return [
        jnp.where(masks[0], kept[plane, at].astype(F32), 0.0)
        + jnp.where(masks[1], got[plane, at].astype(F32), 0.0)
        for plane in range(2)
    ]


def tile_part(shape, cut, rows_in, cols_in, scalars, kept, got, *refs):
    *arrived, out = refs
    fill(shape, cut, 0, rows_in, cols_in, scalars, kept, got, arrived, out)


def fill(shape, cut, first, rows_in, cols_in, scalars, kept, got, arrived, out):
    step = 128
    for start in range(0, out.shape[1], step):
        at = pl.ds(start, step)
        part = part_of(scalars, kept, got, shape, cut, first + start, rows_in, cols_in)
        for plane in range(2):
            for more in arrived:
                part[plane] = part[plane] + more[plane, at].astype(F32)
            out[plane, at] = part[plane].astype(BF16)


def now_parts(shape, cut, scalars, before, kept, got, upper, lower):
    core = scalars[2]
    fill(shape, cut, 0, core, 1 - core, scalars, kept, got, (), upper)
    fill(shape, cut, cut, 1, 0, scalars, kept, got, (), lower)


def own_part(shape, cut, scalars, before, kept, got, upper, lower, third, out):
    fill(shape, cut, 0, 1, 1, scalars, kept, got, (upper, third), out.at[:, :cut])
    fill(shape, cut, cut, 1, 1, scalars, kept, got, (lower,), out.at[:, cut:])


def probe_sum(narrow, scalars, diag, probe_kept, probe_got, *outs):
    me = scalars[4]
    for step, out in enumerate(outs):
        block = lax.rem(me + step, narrow)
        total = probe_kept[block].astype(F32) + probe_got[block].astype(F32)
        out[...] = total.astype(BF16)


def sum_kernel(*refs):
    *terms, out = refs
    total = terms[0][...].astype(F32)
    for term in terms[1:]:
        total = total + term[...].astype(F32)
    out[...] = total.astype(out.dtype)


def scaled_sum(scale, *refs):
    *terms, out = refs
    sum_kernel(*terms, out)
    out[...] = out[...] * scale


def sum_of(*terms):
    return call(
        sum_kernel,
        jax.ShapeDtypeStruct(terms[0].shape, BF16),
        [VMEM] * len(terms),
        8,
        flops=8 * 10**9,
        name="sum",
    )(*terms)


def scatter_parts(x, axis):
    length = lax.axis_size(axis)
    if length > 8:
        return [lax.psum_scatter(x, axis, scatter_dimension=0, tiled=True)[0]]
    me = lax.axis_index(axis)

    def part(of):
        return lax.dynamic_index_in_dim(x, of, 0, keepdims=False)

    terms = [part(me)]
    for step in range(1, length):
        if length & (length - 1):
            pairs = [(i, (i + step) % length) for i in range(length)]
            to = lax.rem(me + step, length)
        else:
            pairs = [(i, i ^ step) for i in range(length)]
            to = me ^ step
        terms.append(lax.ppermute(part(to), axis, pairs))
    return terms


def shards(object_slab, probe_wave, amplitude, row_offset, col_offset, occupied):
    size = probe_wave.shape[1]
    rows, cols = object_slab.shape[1:]
    core = lax.axis_index("probe")
    narrow, wide, cores = (lax.axis_size(name) for name in ("narrow", "wide", "probe"))
    corner = jnp.stack([row_offset[0, 0, 0], col_offset[0, 0, 0]])
    here = [core, occupied[0, 0, 0], lax.axis_index("narrow")]
    scalars = jnp.concatenate([corner, jnp.stack([x.astype(jnp.int32) for x in here])])

    def shape(*dims, dtype=BF16):
        return jax.ShapeDtypeStruct(dims, dtype)

    cut = size // 2
    count = rows - cut
    first = to_neighbour(lax.dynamic_slice_in_dim(object_slab, cut * (1 - core), cut, 1), -1, 0)
    second = to_neighbour(lax.dynamic_slice_in_dim(object_slab, cut * core, count, 1), -1, 0)
    third = to_neighbour(first, -1, 1)
    late_scalars, first_late = lax.optimization_barrier((scalars, first))

    width = size // (narrow * cores)
    table = shape(2, size, size)
    tables = call(
        functools.partial(shift_tables, width),
        (
            (table,) * 5
            + (shape(size, size), shape(size, size))
            + (shape(cols, narrow * width),) * 2
        ),
        [SMEM] + [VMEM] * 6,
        8,
        flops=4 * 10**9,
        bytes_accessed=2 * 10**7,
        name="shift_tables",
    )(late_scalars, *dft_tables(size), probe_wave, amplitude[0, 0, 0])
    second, tables = lax.optimization_barrier((second, tables))
    pieces = (first, swap(first_late), second, swap(second), third, swap(third))
    blocks = shape(narrow, wide, 2, size // wide, width)
    sent, kept, probe_sent, probe_kept = call(
        slot_terms,
        (shape(2, count, cols), shape(2, count, cols), blocks, blocks),
        [SMEM] + [VMEM] * 16,
        18,
        scratch=[pltpu.VMEM((2, size, size), BF16)] * 5
        + [pltpu.VMEM((2, rows, size), BF16), pltpu.VMEM((2, size, size), BF16)],
        flops=6 * 10**9,
        bytes_accessed=2 * 10**7,
        name="slot_terms",
    )(scalars, object_slab, *pieces, *tables)

    got, probe_got = swap(sent), swap(probe_sent)
    scalars = jnp.concatenate([scalars, swap(corner)])

    def tile(name, kernel, height, *more, after=()):
        return call(
            functools.partial(kernel, (rows, size), cut, len(after)),
            shape(2, height, cols),
            [SMEM] + [ANY] * len(after) + [VMEM] * (2 + len(more)),
            8,
            name=name,
        )(scalars, *after, kept, got, *more)

    def diag_part(dims, cut, skip, scalars, *refs):
        tile_part(dims, cut, 0, 0, scalars, *refs[skip:])

    def later_part(dims, cut, skip, scalars, *refs):
        tile_part(dims, cut, 1 - scalars[2], scalars[2], scalars, *refs[skip:])

    diag = tile("diag_part", diag_part, cut)
    from_first = to_neighbour(diag, 1, 0)
    probe_blocks = call(
        functools.partial(probe_sum, narrow),
        (jax.ShapeDtypeStruct(blocks.shape[1:], BF16),) * narrow,
        [SMEM, ANY, VMEM, VMEM],
        8,
        name="probe_sum",
    )(scalars, diag, probe_kept, probe_got)
    upper, lower = call(
        functools.partial(now_parts, (rows, size), cut),
        (shape(2, cut, cols), shape(2, count - cut, cols)),
        [SMEM, ANY, VMEM, VMEM],
        8,
        name="now_parts",
    )(scalars, probe_blocks[0], kept, got)
    from_upper = to_neighbour(upper, 1, 0)
    from_lower = to_neighbour(lower, 1, 0, senders=(1,))
    from_third = to_neighbour(tile("later_part", later_part, cut, from_first), 1, 1)
    received = [
        lax.ppermute(block, "narrow", [(i, (i + step) % narrow) for i in range(narrow)])
        for step, block in enumerate(probe_blocks)
        if step
    ]
    total = sum_of(probe_blocks[0], *received)
    terms = scatter_parts(total, "wide")
    probe_grad = call(
        functools.partial(scaled_sum, 1.0 / math.sqrt(wide * narrow * cores)),
        jax.ShapeDtypeStruct(terms[0].shape, F32),
        [VMEM] * len(terms),
        8,
        flops=20 * 10**9,
        name="probe_grad",
    )(*terms)
    own = call(
        functools.partial(own_part, (rows, size), cut),
        shape(2, count, cols),
        [SMEM, ANY] + [VMEM] * 5,
        8,
        flops=1 * 10**9,
        name="own_part",
    )(scalars, total, kept, got, from_upper, from_lower, from_third)
    other = swap(own)
    object_grad = jnp.where(
        core == 0,
        jnp.concatenate([own[:, :cut], other], 1),
        jnp.concatenate([other[:, :cut], own], 1),
    )
    return (object_grad, probe_grad)


def solution(mesh):
    in_specs = (
        P(None, ("groups", "narrow"), "wide"),
        P(),
        P(("groups", "narrow"), "wide", "probe", None, None),
        P(("groups", "narrow"), "wide", "probe"),
        P(("groups", "narrow"), "wide", "probe"),
        P(("groups", "narrow"), "wide", "probe"),
    )
    out_specs = (
        P(None, ("groups", "narrow"), "wide"),
        P(None, ("groups", "wide"), ("narrow", "probe")),
    )
    return jax.shard_map(shards, mesh=mesh, in_specs=in_specs, out_specs=out_specs, check_vma=False)
```

```python
import functools
import math

import jax
import jax.numpy as jnp
import numpy as np
from jax import lax
from jax.experimental import pallas as pl
from jax.experimental.pallas import tpu as pltpu
from jax.sharding import PartitionSpec as P

BF16 = jnp.bfloat16
F32 = jnp.float32
VMEM = pl.BlockSpec(memory_space=pltpu.VMEM)
SMEM = pl.BlockSpec(memory_space=pltpu.SMEM)
ANY = pl.BlockSpec(memory_space=pl.ANY)


def to_neighbour(x, by, along_narrow, senders=(0, 1)):
    wide, narrow, cores = (lax.axis_size(name) for name in ("wide", "narrow", "probe"))
    pairs = []
    for w in range(wide):
        for n in range(narrow):
            for core in senders:
                w_to, n_to = (w, n + by) if core == along_narrow else (w + by, n)
                if 0 <= w_to < wide and 0 <= n_to < narrow:
                    source = (w * narrow + n) * cores + core
                    pairs.append((source, (w_to * narrow + n_to) * cores + core))
    return lax.ppermute(x, ("wide", "narrow", "probe"), pairs)


def swap(x):
    return lax.ppermute(x, "probe", [(0, 1), (1, 0)])


def halves_first(size):
    return np.concatenate([np.arange(0, size, 2), np.arange(1, size, 2)])


def dft_tables(size):
    product = (np.arange(size)[:, None] * halves_first(size)[None, :]) % size
    angle = product.astype(np.float32) * np.float32(2.0 * math.pi / size)
    norm = np.float32(1.0 / math.sqrt(size))
    pair = (np.cos(angle) * norm, -np.sin(angle) * norm)
    return [jnp.asarray(x, BF16) for x in pair + tuple(x.T for x in pair)]


def dot(a, b):
    return jnp.dot(a, b, preferred_element_type=F32)


def iota(shape, dim):
    return lax.broadcasted_iota(jnp.int32, shape, dim)


def one_hot(equal):
    return jnp.where(equal, 1.0, 0.0).astype(BF16)


def cyclic(at, shift, period):
    back = at - shift
    return jnp.where(back < 0, back + period, back)


def call(kernel, out_shape, in_specs, vmem, scratch=(), flops=0, bytes_accessed=0, name=None):
    return pl.pallas_call(
        kernel,
        out_shape=out_shape,
        in_specs=in_specs,
        out_specs=jax.tree.map(lambda _: VMEM, out_shape),
        scratch_shapes=list(scratch),
        compiler_params=pltpu.CompilerParams(vmem_limit_bytes=vmem * 1024 * 1024),
        cost_estimate=pl.CostEstimate(
            flops=flops, bytes_accessed=bytes_accessed, transcendentals=0
        ),
        name=name,
    )


def shift_tables(
    width, scalars, cos_in, sin_in, cos_t, sin_t, probe_in, amp_in,
    right, right_t, left_t, left, probe, amplitude, back_rows, back_cols, back_cols2,
):
    size = cos_in.shape[0]
    part = size // 2
    row_start, col_start, core = scalars[0], scalars[1], scalars[2]
    row_start = jnp.where(row_start >= size, row_start - size, row_start)
    full = (size, size)

    back_rows[...] = one_hot(cyclic(iota(full, 1), row_start, size) == iota(full, 0))
    count = back_cols.shape[1]
    for out, owner in ((back_cols, core), (back_cols2, 1 - core)):
        at = iota((size, count), 1)
        column = at + (at // width + owner) * width
        out[...] = one_hot(cyclic(iota((size, count), 0), col_start, size) == column)

    for start, table, table_t in ((col_start, right, right_t), (row_start, left_t, left)):
        hot = one_hot(cyclic(iota((part, size), 0), start, size) == iota((part, size), 1))
        hot_t = one_hot(cyclic(iota((size, part), 1), start, size) == iota((size, part), 0))
        cos_part, sin_part = dot(hot, cos_in[...]), dot(hot, sin_in[...])
        cos_turn, sin_turn = dot(cos_t[...], hot_t), dot(sin_t[...], hot_t)
        for odd in range(2):
            at = slice(odd * part, (odd + 1) * part)
            table[odd, :part, :part] = cos_part[:, at].astype(BF16)
            table[odd, part:, part:] = cos_part[:, at].astype(BF16)
            table[odd, :part, part:] = sin_part[:, at].astype(BF16)
            table[odd, part:, :part] = (-sin_part[:, at]).astype(BF16)
            table_t[odd, :part, :part] = cos_turn[at].astype(BF16)
            table_t[odd, part:, part:] = cos_turn[at].astype(BF16)
            table_t[odd, part:, :part] = sin_turn[at].astype(BF16)
            table_t[odd, :part, part:] = (-sin_turn[at]).astype(BF16)

    row_hot = one_hot(cyclic(iota(full, 0), row_start, size) == iota(full, 1))
    col_hot_t = one_hot(cyclic(iota(full, 1), col_start, size) == iota(full, 0))
    for plane in range(2):
        moved = dot(row_hot, probe_in[plane]).astype(BF16)
        probe[plane] = dot(moved, col_hot_t).astype(BF16)

    def frequency(at):
        return jnp.where(at < part, 2 * at, 2 * at - (size - 1))

    moved = dot(one_hot(frequency(iota(full, 0)) == iota(full, 1)), amp_in[...]).astype(BF16)
    amplitude[...] = dot(moved, one_hot(frequency(iota(full, 1)) == iota(full, 0))).astype(BF16)


def slot_terms(
    scalars, own, first, first2, second, second2, third, third2,
    right, right_t, left_t, left, probe, amplitude,
    sent, kept, term, exit_wave, half, chi, back_half, patch, obj,
):
    rows, size = own.shape[1:]
    cut = first.shape[1]
    part = size // 2
    row_start, col_start, core = scalars[0], scalars[1], scalars[2]
    live = scalars[3].astype(F32)
    step = 128
    in_cols = iota((step, size), 1) >= col_start
    core_0 = iota((step, size), 0) * 0 + core == 0

    def tile_value(plane, row):
        def load(on_core_0, on_core_1, at):
            a, b = on_core_0[plane, pl.ds(at, step)], on_core_1[plane, pl.ds(at, step)]
            return jnp.where(core_0, a.astype(F32), b.astype(F32))

        if row < rows:
            here = own[plane, pl.ds(row, step)].astype(F32)
            side = load(first2, first, row) if row < cut else load(second2, second, row - cut)
        elif row - rows < cut:
            here = load(second, second2, row - rows)
            side = load(third2, third, row - rows)
        else:
            here = load(first, first2, row - rows - cut)
            side = load(third, third2, row - rows - cut)
        return jnp.where(in_cols, here, side)

    for start in range(0, size, step):
        at = pl.ds(start, step)
        planes = []
        for plane in range(2):
            row = start
            while row < rows:
                row += size
            value = tile_value(plane, row)
            while row > start:
                row -= size
                in_rows = iota((step, size), 0) + row >= row_start
                value = jnp.where(in_rows, tile_value(plane, row), value)
            patch[plane, at] = value.astype(BF16)
            planes.append(value)
        probe_re, probe_im = probe[0, at].astype(F32), probe[1, at].astype(F32)
        exit_re = probe_re * planes[0] - probe_im * planes[1]
        exit_im = probe_re * planes[1] + probe_im * planes[0]
        for plane, value in ((0, exit_re), (1, exit_im)):
            where = slice(plane * part, (plane + 1) * part)
            exit_wave[0, at, where] = (value[:, :part] + value[:, part:]).astype(BF16)
            exit_wave[1, at, where] = (value[:, :part] - value[:, part:]).astype(BF16)

    for odd in range(2):
        result = dot(exit_wave[odd], right[odd])
        cols = slice(odd * part, (odd + 1) * part)
        for plane in range(2):
            where = slice(plane * part, (plane + 1) * part)
            low, high = result[:part, where], result[part:, where]
            half[0, where, cols] = (low + high).astype(BF16)
            half[1, where, cols] = (low - high).astype(BF16)
    for odd in range(2):
        far = dot(left[odd], half[odd])
        far_re, far_im = far[:part], far[part:]
        magnitude = jnp.sqrt(far_re * far_re + far_im * far_im)
        at = slice(odd * part, (odd + 1) * part)
        factor = (1.0 - amplitude[at].astype(F32) / jnp.maximum(magnitude, 1.0)) * live
        for plane, value in ((0, far_re * factor), (1, far_im * factor)):
            where = slice(plane * part, (plane + 1) * part)
            chi[0, at, where] = value[:, :part].astype(BF16)
            chi[1, at, where] = value[:, part:].astype(BF16)
    for plane in range(2):
        where = slice(plane * part, (plane + 1) * part)
        even, odd = dot(chi[0], right_t[0, :, where]), dot(chi[1], right_t[1, :, where])
        for parity in range(2):
            at = slice(parity * part, (parity + 1) * part)
            back_half[parity, where, :part] = (even[at] + odd[at]).astype(BF16)
            back_half[parity, where, part:] = (even[at] - odd[at]).astype(BF16)
    for start in range(0, size, part):
        at = slice(start, start + part)
        even, odd = dot(left_t[0], back_half[0, :, at]), dot(left_t[1], back_half[1, :, at])
        for lines, back in ((slice(0, part), even + odd), (slice(part, size), even - odd)):
            back_re, back_im = back[:part], back[part:]
            probe_re, probe_im = probe[0, lines, at].astype(F32), probe[1, lines, at].astype(F32)
            obj[0, lines, at] = (probe_re * back_re + probe_im * back_im).astype(BF16)
            obj[1, lines, at] = (probe_re * back_im - probe_im * back_re).astype(BF16)
            patch_re, patch_im = patch[0, lines, at].astype(F32), patch[1, lines, at].astype(F32)
            term[0, lines, at] = (patch_re * back_re + patch_im * back_im).astype(BF16)
            term[1, lines, at] = (patch_re * back_im - patch_im * back_re).astype(BF16)
    count = kept.shape[1]
    for plane in range(2):
        obj[plane, size:] = obj[plane, : obj.shape[1] - size]
        kept[plane] = obj[plane, pl.ds(pl.multiple_of(cut * core, 128), count)]
        sent[plane] = obj[plane, pl.ds(pl.multiple_of(cut * (1 - core), 128), count)]


def probe_parts(term, back_rows, back_cols, back_cols2, probe_sent, probe_kept):
    narrow, blocks, _, height, width = probe_sent.shape
    for plane in range(2):
        moved = dot(back_rows[...], term[plane]).astype(BF16)
        for out, hot in ((probe_sent, back_cols2), (probe_kept, back_cols)):
            result = dot(moved, hot[...]).astype(BF16)
            for column in range(narrow):
                for row in range(blocks):
                    out[column, row, plane] = result[
                        row * height : (row + 1) * height, column * width : (column + 1) * width
                    ]


def part_of(scalars, kept, got, shape, cut, start, rows_in, cols_in):
    rows, size = shape
    step, cols = 128, kept.shape[2]
    below = (1 - rows_in) * (rows - size)
    at = pl.ds(start + below if isinstance(below, int) else pl.multiple_of(start + below, 128), step)
    row_at = iota((step, cols), 0) + (scalars[2] * cut + start + (1 - rows_in) * rows)
    col_at = iota((step, cols), 1)
    masks = []
    for row_start, col_start in ((scalars[0], scalars[1]), (scalars[5], scalars[6])):
        in_cols = jnp.where(col_at >= col_start, 1, 0) == cols_in
        masks.append((row_at >= row_start) & (row_at < row_start + size) & in_cols)
    return [
        jnp.where(masks[0], kept[plane, at].astype(F32), 0.0)
        + jnp.where(masks[1], got[plane, at].astype(F32), 0.0)
        for plane in range(2)
    ]


def tile_part(shape, cut, rows_in, cols_in, scalars, kept, got, *refs):
    *arrived, out = refs
    fill(shape, cut, 0, rows_in, cols_in, scalars, kept, got, arrived, out)


def fill(shape, cut, first, rows_in, cols_in, scalars, kept, got, arrived, out):
    step = 128
    for start in range(0, out.shape[1], step):
        at = pl.ds(start, step)
        part = part_of(scalars, kept, got, shape, cut, first + start, rows_in, cols_in)
        for plane in range(2):
            for more in arrived:
                part[plane] = part[plane] + more[plane, at].astype(F32)
            out[plane, at] = part[plane].astype(BF16)


def now_parts(shape, cut, scalars, before, kept, got, upper, lower):
    core = scalars[2]
    fill(shape, cut, 0, core, 1 - core, scalars, kept, got, (), upper)
    fill(shape, cut, cut, 1, 0, scalars, kept, got, (), lower)


def own_part(shape, cut, scalars, before, kept, got, upper, lower, out):
    fill(shape, cut, 0, 1, 1, scalars, kept, got, (upper,), out.at[:, :cut])
    fill(shape, cut, cut, 1, 1, scalars, kept, got, (lower,), out.at[:, cut:])


def probe_sum(narrow, scalars, diag, probe_kept, probe_got, *outs):
    me = scalars[4]
    for step, out in enumerate(outs):
        block = lax.rem(me + step, narrow)
        total = probe_kept[block].astype(F32) + probe_got[block].astype(F32)
        out[...] = total.astype(BF16)


def sum_kernel(*refs):
    *terms, out = refs
    total = terms[0][...].astype(F32)
    for term in terms[1:]:
        total = total + term[...].astype(F32)
    out[...] = total.astype(out.dtype)


def scaled_sum(scale, *refs):
    *terms, out = refs
    sum_kernel(*terms, out)
    out[...] = out[...] * scale


def sum_of(*terms):
    return call(
        sum_kernel,
        jax.ShapeDtypeStruct(terms[0].shape, BF16),
        [VMEM] * len(terms),
        8,
        flops=8 * 10**9,
        name="sum",
    )(*terms)


def scatter_parts(x, axis):
    length = lax.axis_size(axis)
    if length > 8:
        return [lax.psum_scatter(x, axis, scatter_dimension=0, tiled=True)[0]]
    me = lax.axis_index(axis)

    def part(of):
        return lax.dynamic_index_in_dim(x, of, 0, keepdims=False)

    terms = [part(me)]
    for step in range(1, length):
        if length & (length - 1):
            pairs = [(i, (i + step) % length) for i in range(length)]
            to = lax.rem(me + step, length)
        else:
            pairs = [(i, i ^ step) for i in range(length)]
            to = me ^ step
        terms.append(lax.ppermute(part(to), axis, pairs))
    return terms


def shards(object_slab, probe_wave, amplitude, row_offset, col_offset, occupied):
    size = probe_wave.shape[1]
    rows, cols = object_slab.shape[1:]
    core = lax.axis_index("probe")
    narrow, wide, cores = (lax.axis_size(name) for name in ("narrow", "wide", "probe"))
    corner = jnp.stack([row_offset[0, 0, 0], col_offset[0, 0, 0]])
    here = [core, occupied[0, 0, 0], lax.axis_index("narrow")]
    here = jnp.stack([x.astype(jnp.int32) for x in here])
    scalars = jnp.concatenate([corner, here, swap(corner)])

    def shape(*dims, dtype=BF16):
        return jax.ShapeDtypeStruct(dims, dtype)

    cut = size // 2
    count = rows - cut
    first = to_neighbour(lax.dynamic_slice_in_dim(object_slab, cut * (1 - core), cut, 1), -1, 0)
    second = to_neighbour(lax.dynamic_slice_in_dim(object_slab, cut * core, count, 1), -1, 0)
    third = to_neighbour(first, -1, 1)
    late_scalars, first_late, late_probe, late_amplitude, *late_tables = lax.optimization_barrier(
        (scalars, first, probe_wave, amplitude[0, 0, 0], *dft_tables(size))
    )

    width = size // (narrow * cores)
    table = shape(2, size, size)
    tables = call(
        functools.partial(shift_tables, width),
        (
            (table,) * 5
            + (shape(size, size), shape(size, size))
            + (shape(cols, narrow * width),) * 2
        ),
        [SMEM] + [VMEM] * 6,
        8,
        flops=4 * 10**9,
        bytes_accessed=2 * 10**7,
        name="shift_tables",
    )(late_scalars, *late_tables, late_probe, late_amplitude)
    second, tables = lax.optimization_barrier((second, tables))
    pieces = (first, swap(first_late), second, swap(second), third, swap(third))
    blocks = shape(narrow, wide, 2, size // wide, width)
    *tables, back_rows, back_cols, back_cols2 = tables
    sent, kept, term = call(
        slot_terms,
        (shape(2, count, cols), shape(2, count, cols), table),
        [SMEM] + [VMEM] * 13,
        18,
        scratch=[pltpu.VMEM((2, size, size), BF16)] * 5
        + [pltpu.VMEM((2, rows, size), BF16)],
        flops=6 * 10**9,
        bytes_accessed=2 * 10**7,
        name="slot_terms",
    )(scalars, object_slab, *pieces, *tables)

    probe_sent, probe_kept = call(
        probe_parts, (blocks, blocks), [VMEM] * 4, 8, name="probe_parts"
    )(term, back_rows, back_cols, back_cols2)
    got, probe_got = swap(sent), swap(probe_sent)

    def tile(name, kernel, height, *more, after=()):
        return call(
            functools.partial(kernel, (rows, size), cut, len(after)),
            shape(2, height, cols),
            [SMEM] + [ANY] * len(after) + [VMEM] * (2 + len(more)),
            8,
            name=name,
        )(scalars, *after, kept, got, *more)

    def diag_part(dims, cut, skip, scalars, *refs):
        tile_part(dims, cut, 0, 0, scalars, *refs[skip:])

    def later_part(dims, cut, skip, scalars, *refs):
        tile_part(dims, cut, 1 - scalars[2], scalars[2], scalars, *refs[skip:])

    diag = tile("diag_part", diag_part, cut, after=(probe_sent,))
    from_first = to_neighbour(diag, 1, 0)
    probe_blocks = call(
        functools.partial(probe_sum, narrow),
        (jax.ShapeDtypeStruct(blocks.shape[1:], BF16),) * narrow,
        [SMEM, ANY, VMEM, VMEM],
        8,
        name="probe_sum",
    )(scalars, diag, probe_kept, probe_got)
    upper, lower = call(
        functools.partial(now_parts, (rows, size), cut),
        (shape(2, cut, cols), shape(2, count - cut, cols)),
        [SMEM, ANY, VMEM, VMEM],
        8,
        name="now_parts",
    )(scalars, probe_blocks[0], kept, got)
    from_upper = to_neighbour(upper, 1, 0)
    from_lower = to_neighbour(lower, 1, 0, senders=(1,))
    from_third = to_neighbour(tile("later_part", later_part, cut, from_first), 1, 1)
    received = [
        lax.ppermute(block, "narrow", [(i, (i + step) % narrow) for i in range(narrow)])
        for step, block in enumerate(probe_blocks)
        if step
    ]
    total = sum_of(probe_blocks[0], *received)
    terms = scatter_parts(total, "wide")
    probe_grad = call(
        functools.partial(scaled_sum, 1.0 / math.sqrt(wide * narrow * cores)),
        jax.ShapeDtypeStruct(terms[0].shape, F32),
        [VMEM] * len(terms),
        8,
        flops=20 * 10**9,
        name="probe_grad",
    )(*terms)
    own = call(
        functools.partial(own_part, (rows, size), cut),
        shape(2, count, cols),
        [SMEM, ANY] + [VMEM] * 4,
        8,
        flops=1 * 10**9,
        name="own_part",
    )(scalars, total, kept, got, from_upper, from_lower)
    other, last, other_last = swap(own), from_third, swap(from_third)
    mine = own[:, :cut].astype(F32) + last.astype(F32)
    theirs = other[:, :cut].astype(F32) + other_last.astype(F32)
    object_grad = jnp.concatenate(
        [
            jnp.where(core == 0, mine, theirs).astype(BF16),
            jnp.where(core == 0, theirs, mine).astype(BF16),
            jnp.where(core == 0, other[:, cut:], own[:, cut:]),
        ],
        1,
    )
    return (object_grad, probe_grad)


def solution(mesh):
    in_specs = (
        P(None, ("groups", "narrow"), "wide"),
        P(),
        P(("groups", "narrow"), "wide", "probe", None, None),
        P(("groups", "narrow"), "wide", "probe"),
        P(("groups", "narrow"), "wide", "probe"),
        P(("groups", "narrow"), "wide", "probe"),
    )
    out_specs = (
        P(None, ("groups", "narrow"), "wide"),
        P(None, ("groups", "wide"), ("narrow", "probe")),
    )
    return jax.shard_map(shards, mesh=mesh, in_specs=in_specs, out_specs=out_specs, check_vma=False)
```

```python
import functools
import math

import jax
import jax.numpy as jnp
import numpy as np
from jax import lax
from jax.experimental import pallas as pl
from jax.experimental.pallas import tpu as pltpu
from jax.sharding import PartitionSpec as P

BF16 = jnp.bfloat16
F32 = jnp.float32
VMEM = pl.BlockSpec(memory_space=pltpu.VMEM)
SMEM = pl.BlockSpec(memory_space=pltpu.SMEM)
ANY = pl.BlockSpec(memory_space=pl.ANY)


def to_neighbour(x, by, along_narrow, senders=(0, 1)):
    wide, narrow, cores = (lax.axis_size(name) for name in ("wide", "narrow", "probe"))
    pairs = []
    for w in range(wide):
        for n in range(narrow):
            for role in senders:
                core = 1 - role
                w_to, n_to = (w, n + by) if role == along_narrow else (w + by, n)
                if 0 <= w_to < wide and 0 <= n_to < narrow:
                    source = (w * narrow + n) * cores + core
                    pairs.append((source, (w_to * narrow + n_to) * cores + core))
    return lax.ppermute(x, ("wide", "narrow", "probe"), pairs)


def swap(x):
    return lax.ppermute(x, "probe", [(0, 1), (1, 0)])


def halves_first(size):
    return np.concatenate([np.arange(0, size, 2), np.arange(1, size, 2)])


def dft_tables(size):
    product = (np.arange(size)[:, None] * halves_first(size)[None, :]) % size
    angle = product.astype(np.float32) * np.float32(2.0 * math.pi / size)
    norm = np.float32(1.0 / math.sqrt(size))
    pair = (np.cos(angle) * norm, -np.sin(angle) * norm)
    return jnp.asarray(np.stack(pair + tuple(x.T for x in pair)), BF16)


def dot(a, b):
    return jnp.dot(a, b, preferred_element_type=F32)


def iota(shape, dim):
    return lax.broadcasted_iota(jnp.int32, shape, dim)


def one_hot(equal):
    return jnp.where(equal, 1.0, 0.0).astype(BF16)


def cyclic(at, shift, period):
    back = at - shift
    return jnp.where(back < 0, back + period, back)


def call(kernel, out_shape, in_specs, vmem, scratch=(), flops=0, bytes_accessed=0, name=None):
    return pl.pallas_call(
        kernel,
        out_shape=out_shape,
        in_specs=in_specs,
        out_specs=jax.tree.map(lambda _: VMEM, out_shape),
        scratch_shapes=list(scratch),
        compiler_params=pltpu.CompilerParams(vmem_limit_bytes=vmem * 1024 * 1024),
        cost_estimate=pl.CostEstimate(
            flops=flops, bytes_accessed=bytes_accessed, transcendentals=0
        ),
        name=name,
    )


def shift_tables(
    width, scalars, dft, probe_in, amp_in, first_in, before,
    right, right_t, left_t, left, probe, amplitude, back_rows, back_cols, back_cols2, first,
):
    size = dft.shape[1]
    part = size // 2
    first[...] = first_in[...]
    row_start, col_start, core = scalars[0], scalars[1], scalars[2]
    row_start = jnp.where(row_start >= size, row_start - size, row_start)
    full = (size, size)

    back_rows[...] = one_hot(cyclic(iota(full, 1), row_start, size) == iota(full, 0))
    count = back_cols.shape[1]
    for out, owner in ((back_cols, 1 - core), (back_cols2, core)):
        at = iota((size, count), 1)
        column = at + (at // width + owner) * width
        out[...] = one_hot(cyclic(iota((size, count), 0), col_start, size) == column)

    for start, table, table_t in ((col_start, right, right_t), (row_start, left_t, left)):
        hot = one_hot(cyclic(iota((part, size), 0), start, size) == iota((part, size), 1))
        hot_t = one_hot(cyclic(iota((size, part), 1), start, size) == iota((size, part), 0))
        cos_part, sin_part = dot(hot, dft[0]), dot(hot, dft[1])
        cos_turn, sin_turn = dot(dft[2], hot_t), dot(dft[3], hot_t)
        for odd in range(2):
            at = slice(odd * part, (odd + 1) * part)
            table[odd, :part, :part] = cos_part[:, at].astype(BF16)
            table[odd, part:, part:] = cos_part[:, at].astype(BF16)
            table[odd, :part, part:] = sin_part[:, at].astype(BF16)
            table[odd, part:, :part] = (-sin_part[:, at]).astype(BF16)
            table_t[odd, :part, :part] = cos_turn[at].astype(BF16)
            table_t[odd, part:, part:] = cos_turn[at].astype(BF16)
            table_t[odd, part:, :part] = sin_turn[at].astype(BF16)
            table_t[odd, :part, part:] = (-sin_turn[at]).astype(BF16)

    row_hot = one_hot(cyclic(iota(full, 0), row_start, size) == iota(full, 1))
    col_hot_t = one_hot(cyclic(iota(full, 1), col_start, size) == iota(full, 0))
    for plane in range(2):
        moved = dot(row_hot, probe_in[plane]).astype(BF16)
        probe[plane] = dot(moved, col_hot_t).astype(BF16)

    def frequency(at):
        return jnp.where(at < part, 2 * at, 2 * at - (size - 1))

    moved = dot(one_hot(frequency(iota(full, 0)) == iota(full, 1)), amp_in[...]).astype(BF16)
    amplitude[...] = dot(moved, one_hot(frequency(iota(full, 1)) == iota(full, 0))).astype(BF16)


def first_rows(slab, out, second):
    core = 1 - lax.axis_index("probe")
    count = out.shape[1]
    out[...] = slab[:, pl.ds(pl.multiple_of(count * (1 - core), 128), count)]
    second[...] = slab[:, pl.ds(pl.multiple_of(count * core, 128), second.shape[1])]


def slot_terms(
    scalars, own, first, first2, second, second2, third, third2,
    right, right_t, left_t, left, probe, amplitude,
    sent, kept, term, exit_wave, half, chi, back_half, patch, obj,
):
    rows, size = own.shape[1:]
    cut = first.shape[1]
    part = size // 2
    row_start, col_start, core = scalars[0], scalars[1], scalars[2]
    live = scalars[3].astype(F32)
    step = 128
    in_cols = iota((step, size), 1) >= col_start
    core_0 = iota((step, size), 0) * 0 + core == 0

    def tile_value(plane, row):
        def load(on_core_0, on_core_1, at):
            a, b = on_core_0[plane, pl.ds(at, step)], on_core_1[plane, pl.ds(at, step)]
            return jnp.where(core_0, a.astype(F32), b.astype(F32))

        if row < rows:
            here = own[plane, pl.ds(row, step)].astype(F32)
            side = load(first2, first, row) if row < cut else load(second2, second, row - cut)
        elif row - rows < cut:
            here = load(second, second2, row - rows)
            side = load(third2, third, row - rows)
        else:
            here = load(first, first2, row - rows - cut)
            side = load(third, third2, row - rows - cut)
        return jnp.where(in_cols, here, side)

    for start in range(0, size, step):
        at = pl.ds(start, step)
        planes = []
        for plane in range(2):
            row = start
            while row < rows:
                row += size
            value = tile_value(plane, row)
            while row > start:
                row -= size
                in_rows = iota((step, size), 0) + row >= row_start
                value = jnp.where(in_rows, tile_value(plane, row), value)
            patch[plane, at] = value.astype(BF16)
            planes.append(value)
        probe_re, probe_im = probe[0, at].astype(F32), probe[1, at].astype(F32)
        exit_re = probe_re * planes[0] - probe_im * planes[1]
        exit_im = probe_re * planes[1] + probe_im * planes[0]
        for plane, value in ((0, exit_re), (1, exit_im)):
            where = slice(plane * part, (plane + 1) * part)
            exit_wave[0, at, where] = (value[:, :part] + value[:, part:]).astype(BF16)
            exit_wave[1, at, where] = (value[:, :part] - value[:, part:]).astype(BF16)

    for odd in range(2):
        result = dot(exit_wave[odd], right[odd])
        cols = slice(odd * part, (odd + 1) * part)
        for plane in range(2):
            where = slice(plane * part, (plane + 1) * part)
            low, high = result[:part, where], result[part:, where]
            half[0, where, cols] = (low + high).astype(BF16)
            half[1, where, cols] = (low - high).astype(BF16)
    for odd in range(2):
        far = dot(left[odd], half[odd])
        far_re, far_im = far[:part], far[part:]
        magnitude = jnp.sqrt(far_re * far_re + far_im * far_im)
        at = slice(odd * part, (odd + 1) * part)
        factor = (1.0 - amplitude[at].astype(F32) / jnp.maximum(magnitude, 1.0)) * live
        for plane, value in ((0, far_re * factor), (1, far_im * factor)):
            where = slice(plane * part, (plane + 1) * part)
            chi[0, at, where] = value[:, :part].astype(BF16)
            chi[1, at, where] = value[:, part:].astype(BF16)
    for plane in range(2):
        where = slice(plane * part, (plane + 1) * part)
        even, odd = dot(chi[0], right_t[0, :, where]), dot(chi[1], right_t[1, :, where])
        for parity in range(2):
            at = slice(parity * part, (parity + 1) * part)
            back_half[parity, where, :part] = (even[at] + odd[at]).astype(BF16)
            back_half[parity, where, part:] = (even[at] - odd[at]).astype(BF16)
    for start in range(0, size, part):
        at = slice(start, start + part)
        even, odd = dot(left_t[0], back_half[0, :, at]), dot(left_t[1], back_half[1, :, at])
        for lines, back in ((slice(0, part), even + odd), (slice(part, size), even - odd)):
            back_re, back_im = back[:part], back[part:]
            probe_re, probe_im = probe[0, lines, at].astype(F32), probe[1, lines, at].astype(F32)
            obj[0, lines, at] = (probe_re * back_re + probe_im * back_im).astype(BF16)
            obj[1, lines, at] = (probe_re * back_im - probe_im * back_re).astype(BF16)
            patch_re, patch_im = patch[0, lines, at].astype(F32), patch[1, lines, at].astype(F32)
            term[0, lines, at] = (patch_re * back_re + patch_im * back_im).astype(BF16)
            term[1, lines, at] = (patch_re * back_im - patch_im * back_re).astype(BF16)
    count = kept.shape[1]
    for plane in range(2):
        obj[plane, size:] = obj[plane, : obj.shape[1] - size]
        kept[plane] = obj[plane, pl.ds(pl.multiple_of(cut * core, 128), count)]
        sent[plane] = obj[plane, pl.ds(pl.multiple_of(cut * (1 - core), 128), count)]


def probe_parts(term, back_rows, back_cols, back_cols2, probe_sent, probe_kept):
    narrow, blocks, _, height, width = probe_sent.shape
    for plane in range(2):
        moved = dot(back_rows[...], term[plane]).astype(BF16)
        for out, hot in ((probe_sent, back_cols2), (probe_kept, back_cols)):
            result = dot(moved, hot[...]).astype(BF16)
            for column in range(narrow):
                for row in range(blocks):
                    out[column, row, plane] = result[
                        row * height : (row + 1) * height, column * width : (column + 1) * width
                    ]


def part_of(scalars, kept, got, shape, cut, start, rows_in, cols_in):
    rows, size = shape
    step, cols = 128, kept.shape[2]
    below = (1 - rows_in) * (rows - size)
    at = pl.ds(start + below if isinstance(below, int) else pl.multiple_of(start + below, 128), step)
    row_at = iota((step, cols), 0) + (scalars[2] * cut + start + (1 - rows_in) * rows)
    col_at = iota((step, cols), 1)
    masks = []
    for row_start, col_start in ((scalars[0], scalars[1]), (scalars[5], scalars[6])):
        in_cols = jnp.where(col_at >= col_start, 1, 0) == cols_in
        masks.append((row_at >= row_start) & (row_at < row_start + size) & in_cols)
    return [
        jnp.where(masks[0], kept[plane, at].astype(F32), 0.0)
        + jnp.where(masks[1], got[plane, at].astype(F32), 0.0)
        for plane in range(2)
    ]


def tile_part(shape, cut, rows_in, cols_in, scalars, kept, got, *refs):
    *arrived, out = refs
    fill(shape, cut, 0, rows_in, cols_in, scalars, kept, got, arrived, out)


def fill(shape, cut, first, rows_in, cols_in, scalars, kept, got, arrived, out):
    step = 128
    for start in range(0, out.shape[1], step):
        at = pl.ds(start, step)
        part = part_of(scalars, kept, got, shape, cut, first + start, rows_in, cols_in)
        for plane in range(2):
            for more in arrived:
                part[plane] = part[plane] + more[plane, at].astype(F32)
            out[plane, at] = part[plane].astype(BF16)


def now_parts(shape, cut, scalars, before, kept, got, upper, lower):
    core = scalars[2]
    fill(shape, cut, 0, core, 1 - core, scalars, kept, got, (), upper)
    fill(shape, cut, cut, 1, 0, scalars, kept, got, (), lower)


def own_part(shape, cut, scalars, before, kept, got, upper, lower, out):
    fill(shape, cut, 0, 1, 1, scalars, kept, got, (upper,), out.at[:, :cut])
    fill(shape, cut, cut, 1, 1, scalars, kept, got, (lower,), out.at[:, cut:])


def probe_sum(narrow, scalars, diag, probe_kept, probe_got, *outs):
    me = scalars[4]
    for step, out in enumerate(outs):
        block = lax.rem(me + step, narrow)
        total = probe_kept[block].astype(F32) + probe_got[block].astype(F32)
        out[...] = total.astype(BF16)


def sum_kernel(*refs):
    *terms, out = refs
    total = terms[0][...].astype(F32)
    for term in terms[1:]:
        total = total + term[...].astype(F32)
    out[...] = total.astype(out.dtype)


def scaled_sum(scale, *refs):
    *terms, out = refs
    sum_kernel(*terms, out)
    out[...] = out[...] * scale


def sum_of(*terms):
    return call(
        sum_kernel,
        jax.ShapeDtypeStruct(terms[0].shape, BF16),
        [VMEM] * len(terms),
        8,
        flops=8 * 10**9,
        name="sum",
    )(*terms)


def scatter_parts(x, axis):
    length = lax.axis_size(axis)
    if length > 8:
        return [lax.psum_scatter(x, axis, scatter_dimension=0, tiled=True)[0]]
    me = lax.axis_index(axis)

    def part(of):
        return lax.dynamic_index_in_dim(x, of, 0, keepdims=False)

    terms = [part(me)]
    for step in range(1, length):
        if length & (length - 1):
            pairs = [(i, (i + step) % length) for i in range(length)]
            to = lax.rem(me + step, length)
        else:
            pairs = [(i, i ^ step) for i in range(length)]
            to = me ^ step
        terms.append(lax.ppermute(part(to), axis, pairs))
    return terms


def shards(object_slab, probe_wave, amplitude, row_offset, col_offset, occupied):
    size = probe_wave.shape[1]
    rows, cols = object_slab.shape[1:]
    core = 1 - lax.axis_index("probe")
    narrow, wide, cores = (lax.axis_size(name) for name in ("narrow", "wide", "probe"))
    corner = jnp.stack([row_offset[0, 0, 0], col_offset[0, 0, 0]])
    here = [core, occupied[0, 0, 0], lax.axis_index("narrow")]
    here = jnp.stack([x.astype(jnp.int32) for x in here])
    scalars = jnp.concatenate([corner, here, swap(corner)])

    def shape(*dims, dtype=BF16):
        return jax.ShapeDtypeStruct(dims, dtype)

    cut = size // 2
    count = rows - cut
    start, more = call(
        first_rows, (shape(2, cut, cols), shape(2, count, cols)), [VMEM], 8, name="first_rows"
    )(object_slab)
    first = to_neighbour(start, -1, 0)
    second = to_neighbour(more, -1, 0)
    third = to_neighbour(first, -1, 1)
    late_scalars, first_late, late_probe, late_amplitude, late_tables = lax.optimization_barrier(
        (scalars, first, probe_wave, amplitude[0, 0, 0], dft_tables(size))
    )

    first2 = swap(first_late)
    width = size // (narrow * cores)
    table = shape(2, size, size)
    *tables, first_kept = call(
        functools.partial(shift_tables, width),
        (
            (table,) * 5
            + (shape(size, size), shape(size, size))
            + (shape(cols, narrow * width),) * 2
            + (shape(2, cut, cols),)
        ),
        [SMEM] + [VMEM] * 4 + [ANY],
        8,
        flops=0 * 10**9,
        name="shift_tables",
    )(late_scalars, late_tables, late_probe, late_amplitude, first_late, first2)
    second, tables = lax.optimization_barrier((second, tables))
    pieces = (first_kept, first2, second, swap(second), third, swap(third))
    blocks = shape(narrow, wide, 2, size // wide, width)
    *tables, back_rows, back_cols, back_cols2 = tables
    sent, kept, term = call(
        slot_terms,
        (shape(2, count, cols), shape(2, count, cols), table),
        [SMEM] + [VMEM] * 13,
        18,
        scratch=[pltpu.VMEM((2, size, size), BF16)] * 5
        + [pltpu.VMEM((2, rows, size), BF16)],
        flops=6 * 10**9,
        bytes_accessed=2 * 10**7,
        name="slot_terms",
    )(scalars, object_slab, *pieces, *tables)

    probe_sent, probe_kept = call(
        probe_parts, (blocks, blocks), [VMEM] * 4, 8, name="probe_parts"
    )(term, back_rows, back_cols, back_cols2)
    got, probe_got = swap(sent), swap(probe_sent)

    def tile(name, kernel, height, *more, after=()):
        return call(
            functools.partial(kernel, (rows, size), cut, len(after)),
            shape(2, height, cols),
            [SMEM] + [ANY] * len(after) + [VMEM] * (2 + len(more)),
            8,
            name=name,
        )(scalars, *after, kept, got, *more)

    def diag_part(dims, cut, skip, scalars, *refs):
        tile_part(dims, cut, 0, 0, scalars, *refs[skip:])

    def later_part(dims, cut, skip, scalars, *refs):
        tile_part(dims, cut, 1 - scalars[2], scalars[2], scalars, *refs[skip:])

    diag = tile("diag_part", diag_part, cut, after=(probe_sent,))
    from_first = to_neighbour(diag, 1, 0)
    probe_blocks = call(
        functools.partial(probe_sum, narrow),
        (jax.ShapeDtypeStruct(blocks.shape[1:], BF16),) * narrow,
        [SMEM, ANY, VMEM, VMEM],
        8,
        name="probe_sum",
    )(scalars, diag, probe_kept, probe_got)
    upper, lower = call(
        functools.partial(now_parts, (rows, size), cut),
        (shape(2, cut, cols), shape(2, count - cut, cols)),
        [SMEM, ANY, VMEM, VMEM],
        8,
        name="now_parts",
    )(scalars, probe_blocks[0], kept, got)
    from_upper = to_neighbour(upper, 1, 0)
    from_lower = to_neighbour(lower, 1, 0, senders=(1,))
    from_third = to_neighbour(tile("later_part", later_part, cut, from_first), 1, 1)
    received = [
        lax.ppermute(block, "narrow", [(i, (i + step) % narrow) for i in range(narrow)])
        for step, block in enumerate(probe_blocks)
        if step
    ]
    total = sum_of(probe_blocks[0], *received)
    terms = scatter_parts(total, "wide")
    probe_grad = call(
        functools.partial(scaled_sum, 1.0 / math.sqrt(wide * narrow * cores)),
        jax.ShapeDtypeStruct(terms[0].shape, F32),
        [VMEM] * len(terms),
        8,
        flops=20 * 10**9,
        name="probe_grad",
    )(*terms)
    own = call(
        functools.partial(own_part, (rows, size), cut),
        shape(2, count, cols),
        [SMEM, ANY] + [VMEM] * 4,
        8,
        flops=1 * 10**9,
        name="own_part",
    )(scalars, total, kept, got, from_upper, from_lower)
    other, last, other_last = swap(own), from_third, swap(from_third)
    mine = own[:, :cut].astype(F32) + last.astype(F32)
    theirs = other[:, :cut].astype(F32) + other_last.astype(F32)
    object_grad = jnp.concatenate(
        [
            jnp.where(core == 0, mine, theirs).astype(BF16),
            jnp.where(core == 0, theirs, mine).astype(BF16),
            jnp.where(core == 0, other[:, cut:], own[:, cut:]),
        ],
        1,
    )
    return (object_grad, probe_grad)


def solution(mesh):
    in_specs = (
        P(None, ("groups", "narrow"), "wide"),
        P(),
        P(("groups", "narrow"), "wide", "probe", None, None),
        P(("groups", "narrow"), "wide", "probe"),
        P(("groups", "narrow"), "wide", "probe"),
        P(("groups", "narrow"), "wide", "probe"),
    )
    out_specs = (
        P(None, ("groups", "narrow"), "wide"),
        P(None, ("groups", "wide"), ("narrow", "probe")),
    )
    return jax.shard_map(shards, mesh=mesh, in_specs=in_specs, out_specs=out_specs, check_vma=False)
```

```python
import functools
import math

import jax
import jax.numpy as jnp
import numpy as np
from jax import lax
from jax.experimental import pallas as pl
from jax.experimental.pallas import tpu as pltpu
from jax.sharding import PartitionSpec as P

BF16 = jnp.bfloat16
F32 = jnp.float32
VMEM = pl.BlockSpec(memory_space=pltpu.VMEM)
SMEM = pl.BlockSpec(memory_space=pltpu.SMEM)
ANY = pl.BlockSpec(memory_space=pl.ANY)


def to_neighbour(x, by, along_narrow, senders=(0, 1)):
    wide, narrow, cores = (lax.axis_size(name) for name in ("wide", "narrow", "probe"))
    pairs = []
    for w in range(wide):
        for n in range(narrow):
            for role in senders:
                core = 1 - role
                w_to, n_to = (w, n + by) if role == along_narrow else (w + by, n)
                if 0 <= w_to < wide and 0 <= n_to < narrow:
                    source = (w * narrow + n) * cores + core
                    pairs.append((source, (w_to * narrow + n_to) * cores + core))
    return lax.ppermute(x, ("wide", "narrow", "probe"), pairs)


def swap(x):
    return lax.ppermute(x, "probe", [(0, 1), (1, 0)])


def halves_first(size):
    return np.concatenate([np.arange(0, size, 2), np.arange(1, size, 2)])


def dft_tables(size):
    product = (np.arange(size)[:, None] * halves_first(size)[None, :]) % size
    angle = product.astype(np.float32) * np.float32(2.0 * math.pi / size)
    norm = np.float32(1.0 / math.sqrt(size))
    pair = (np.cos(angle) * norm, -np.sin(angle) * norm)
    return jnp.asarray(np.stack(pair + tuple(x.T for x in pair)), BF16)


def dot(a, b):
    return jnp.dot(a, b, preferred_element_type=F32)


def rounded(x):
    return x.astype(BF16).astype(F32)


def iota(shape, dim):
    return lax.broadcasted_iota(jnp.int32, shape, dim)


def one_hot(equal):
    return jnp.where(equal, 1.0, 0.0).astype(BF16)


def cyclic(at, shift, period):
    back = at - shift
    return jnp.where(back < 0, back + period, back)


def call(kernel, out_shape, in_specs, vmem, scratch=(), flops=0, bytes_accessed=0, name=None):
    return pl.pallas_call(
        kernel,
        out_shape=out_shape,
        in_specs=in_specs,
        out_specs=jax.tree.map(lambda _: VMEM, out_shape),
        scratch_shapes=list(scratch),
        compiler_params=pltpu.CompilerParams(vmem_limit_bytes=vmem * 1024 * 1024),
        cost_estimate=pl.CostEstimate(
            flops=flops, bytes_accessed=bytes_accessed, transcendentals=0
        ),
        name=name,
    )


def shift_tables(
    width, scalars, dft, probe_in, amp_in, first_in, before,
    right, right_t, left_t, left, probe, amplitude, back_rows, back_cols, back_cols2, first,
):
    size = dft.shape[1]
    part = size // 2
    first[...] = first_in[...]
    row_start, col_start, core = scalars[0], scalars[1], scalars[2]
    row_start = jnp.where(row_start >= size, row_start - size, row_start)
    full = (size, size)

    back_rows[...] = one_hot(cyclic(iota(full, 1), row_start, size) == iota(full, 0))
    count = back_cols.shape[1]
    for out, owner in ((back_cols, 1 - core), (back_cols2, core)):
        at = iota((size, count), 1)
        column = at + (at // width + owner) * width
        out[...] = one_hot(cyclic(iota((size, count), 0), col_start, size) == column)

    for start, table, table_t in ((col_start, right, right_t), (row_start, left_t, left)):
        hot = one_hot(cyclic(iota((part, size), 0), start, size) == iota((part, size), 1))
        hot_t = one_hot(cyclic(iota((size, part), 1), start, size) == iota((size, part), 0))
        cos_part, sin_part = dot(hot, dft[0]), dot(hot, dft[1])
        cos_turn, sin_turn = dot(dft[2], hot_t), dot(dft[3], hot_t)
        for odd in range(2):
            at = slice(odd * part, (odd + 1) * part)
            table[odd, :part, :part] = cos_part[:, at].astype(BF16)
            table[odd, part:, part:] = cos_part[:, at].astype(BF16)
            table[odd, :part, part:] = sin_part[:, at].astype(BF16)
            table[odd, part:, :part] = (-sin_part[:, at]).astype(BF16)
            table_t[odd, :part, :part] = cos_turn[at].astype(BF16)
            table_t[odd, part:, part:] = cos_turn[at].astype(BF16)
            table_t[odd, part:, :part] = sin_turn[at].astype(BF16)
            table_t[odd, :part, part:] = (-sin_turn[at]).astype(BF16)

    row_hot = one_hot(cyclic(iota(full, 0), row_start, size) == iota(full, 1))
    col_hot_t = one_hot(cyclic(iota(full, 1), col_start, size) == iota(full, 0))
    for plane in range(2):
        moved = dot(row_hot, probe_in[plane]).astype(BF16)
        probe[plane] = dot(moved, col_hot_t).astype(BF16)

    def frequency(at):
        return jnp.where(at < part, 2 * at, 2 * at - (size - 1))

    moved = dot(one_hot(frequency(iota(full, 0)) == iota(full, 1)), amp_in[...]).astype(BF16)
    amplitude[...] = dot(moved, one_hot(frequency(iota(full, 1)) == iota(full, 0))).astype(BF16)


def first_rows(slab, out, second):
    core = 1 - lax.axis_index("probe")
    count = out.shape[1]
    out[...] = slab[:, pl.ds(pl.multiple_of(count * (1 - core), 128), count)]
    second[...] = slab[:, pl.ds(pl.multiple_of(count * core, 128), second.shape[1])]


def slot_terms(
    scalars, own, first, first2, second, second2, third, third2,
    right, right_t, left_t, left, probe, amplitude,
    sent, kept, term, exit_wave, half, chi, back_half, patch, obj,
):
    rows, size = own.shape[1:]
    cut = first.shape[1]
    part = size // 2
    row_start, col_start, core = scalars[0], scalars[1], scalars[2]
    live = scalars[3].astype(F32)
    step = 128
    in_cols = iota((step, size), 1) >= col_start
    core_0 = iota((step, size), 0) * 0 + core == 0

    def tile_value(plane, row):
        def load(on_core_0, on_core_1, at):
            a, b = on_core_0[plane, pl.ds(at, step)], on_core_1[plane, pl.ds(at, step)]
            return jnp.where(core_0, a.astype(F32), b.astype(F32))

        if row < rows:
            here = own[plane, pl.ds(row, step)].astype(F32)
            side = load(first2, first, row) if row < cut else load(second2, second, row - cut)
        elif row - rows < cut:
            here = load(second, second2, row - rows)
            side = load(third2, third, row - rows)
        else:
            here = load(first, first2, row - rows - cut)
            side = load(third, third2, row - rows - cut)
        return jnp.where(in_cols, here, side)

    for start in range(0, size, step):
        at = pl.ds(start, step)
        planes = []
        for plane in range(2):
            row = start
            while row < rows:
                row += size
            value = tile_value(plane, row)
            while row > start:
                row -= size
                in_rows = iota((step, size), 0) + row >= row_start
                value = jnp.where(in_rows, tile_value(plane, row), value)
            patch[plane, at] = value.astype(BF16)
            planes.append(value)
        probe_re, probe_im = probe[0, at].astype(F32), probe[1, at].astype(F32)
        exit_re = probe_re * planes[0] - probe_im * planes[1]
        exit_im = probe_re * planes[1] + probe_im * planes[0]
        for plane, value in ((0, rounded(exit_re)), (1, rounded(exit_im))):
            where = slice(plane * part, (plane + 1) * part)
            exit_wave[0, at, where] = (value[:, :part] + value[:, part:]).astype(BF16)
            exit_wave[1, at, where] = (value[:, :part] - value[:, part:]).astype(BF16)

    for odd in range(2):
        result = rounded(dot(exit_wave[odd], right[odd]))
        cols = slice(odd * part, (odd + 1) * part)
        for plane in range(2):
            where = slice(plane * part, (plane + 1) * part)
            low, high = result[:part, where], result[part:, where]
            half[0, where, cols] = (low + high).astype(BF16)
            half[1, where, cols] = (low - high).astype(BF16)
    for odd in range(2):
        far = dot(left[odd], half[odd])
        far_re, far_im = far[:part], far[part:]
        magnitude = jnp.sqrt(far_re * far_re + far_im * far_im)
        at = slice(odd * part, (odd + 1) * part)
        factor = (1.0 - amplitude[at].astype(F32) / jnp.maximum(magnitude, 1.0)) * live
        for plane, value in ((0, far_re * factor), (1, far_im * factor)):
            where = slice(plane * part, (plane + 1) * part)
            chi[0, at, where] = value[:, :part].astype(BF16)
            chi[1, at, where] = value[:, part:].astype(BF16)
    for plane in range(2):
        where = slice(plane * part, (plane + 1) * part)
        even, odd = dot(chi[0], right_t[0, :, where]), dot(chi[1], right_t[1, :, where])
        for parity in range(2):
            at = slice(parity * part, (parity + 1) * part)
            back_half[parity, where, :part] = (even[at] + odd[at]).astype(BF16)
            back_half[parity, where, part:] = (even[at] - odd[at]).astype(BF16)
    for start in range(0, size, part):
        at = slice(start, start + part)
        even, odd = dot(left_t[0], back_half[0, :, at]), dot(left_t[1], back_half[1, :, at])
        for lines, back in ((slice(0, part), even + odd), (slice(part, size), even - odd)):
            back_re, back_im = back[:part], back[part:]
            probe_re, probe_im = probe[0, lines, at].astype(F32), probe[1, lines, at].astype(F32)
            obj[0, lines, at] = (probe_re * back_re + probe_im * back_im).astype(BF16)
            obj[1, lines, at] = (probe_re * back_im - probe_im * back_re).astype(BF16)
            patch_re, patch_im = patch[0, lines, at].astype(F32), patch[1, lines, at].astype(F32)
            term[0, lines, at] = (patch_re * back_re + patch_im * back_im).astype(BF16)
            term[1, lines, at] = (patch_re * back_im - patch_im * back_re).astype(BF16)
    count = kept.shape[1]
    for plane in range(2):
        obj[plane, size:] = obj[plane, : obj.shape[1] - size]
        kept[plane] = obj[plane, pl.ds(pl.multiple_of(cut * core, 128), count)]
        sent[plane] = obj[plane, pl.ds(pl.multiple_of(cut * (1 - core), 128), count)]


def probe_parts(term, back_rows, back_cols, back_cols2, probe_sent, probe_kept):
    narrow, blocks, _, height, width = probe_sent.shape
    for plane in range(2):
        moved = dot(back_rows[...], term[plane]).astype(BF16)
        for out, hot in ((probe_sent, back_cols2), (probe_kept, back_cols)):
            result = dot(moved, hot[...]).astype(BF16)
            for column in range(narrow):
                for row in range(blocks):
                    out[column, row, plane] = result[
                        row * height : (row + 1) * height, column * width : (column + 1) * width
                    ]


def part_of(scalars, kept, got, shape, cut, start, rows_in, cols_in):
    rows, size = shape
    step, cols = 128, kept.shape[2]
    below = (1 - rows_in) * (rows - size)
    at = pl.ds(start + below if isinstance(below, int) else pl.multiple_of(start + below, 128), step)
    row_at = iota((step, cols), 0) + (scalars[2] * cut + start + (1 - rows_in) * rows)
    col_at = iota((step, cols), 1)
    masks = []
    for row_start, col_start in ((scalars[0], scalars[1]), (scalars[5], scalars[6])):
        in_cols = jnp.where(col_at >= col_start, 1, 0) == cols_in
        masks.append((row_at >= row_start) & (row_at < row_start + size) & in_cols)
    return [
        jnp.where(masks[0], kept[plane, at].astype(F32), 0.0)
        + jnp.where(masks[1], got[plane, at].astype(F32), 0.0)
        for plane in range(2)
    ]


def tile_part(shape, cut, rows_in, cols_in, scalars, kept, got, *refs):
    *arrived, out = refs
    fill(shape, cut, 0, rows_in, cols_in, scalars, kept, got, arrived, out)


def fill(shape, cut, first, rows_in, cols_in, scalars, kept, got, arrived, out):
    step = 128
    for start in range(0, out.shape[1], step):
        at = pl.ds(start, step)
        part = part_of(scalars, kept, got, shape, cut, first + start, rows_in, cols_in)
        for plane in range(2):
            for more in arrived:
                part[plane] = part[plane] + more[plane, at].astype(F32)
            out[plane, at] = part[plane].astype(BF16)


def now_parts(shape, cut, scalars, before, kept, got, upper, lower):
    core = scalars[2]
    fill(shape, cut, 0, core, 1 - core, scalars, kept, got, (), upper)
    fill(shape, cut, cut, 1, 0, scalars, kept, got, (), lower)


def own_part(shape, cut, scalars, before, kept, got, upper, lower, out):
    fill(shape, cut, 0, 1, 1, scalars, kept, got, (upper,), out.at[:, :cut])
    fill(shape, cut, cut, 1, 1, scalars, kept, got, (lower,), out.at[:, cut:])


def probe_sum(narrow, scalars, diag, probe_kept, probe_got, *outs):
    me = scalars[4]
    for step, out in enumerate(outs):
        block = lax.rem(me + step, narrow)
        total = probe_kept[block].astype(F32) + probe_got[block].astype(F32)
        out[...] = total.astype(BF16)


def sum_kernel(*refs):
    *terms, out = refs
    total = terms[0][...].astype(F32)
    for term in terms[1:]:
        total = total + term[...].astype(F32)
    out[...] = total.astype(out.dtype)


def scaled_sum(scale, *refs):
    *terms, out = refs
    sum_kernel(*terms, out)
    out[...] = out[...] * scale


def sum_of(*terms):
    return call(
        sum_kernel,
        jax.ShapeDtypeStruct(terms[0].shape, BF16),
        [VMEM] * len(terms),
        8,
        flops=8 * 10**9,
        name="sum",
    )(*terms)


def scatter_parts(x, axis):
    length = lax.axis_size(axis)
    if length > 8:
        return [lax.psum_scatter(x, axis, scatter_dimension=0, tiled=True)[0]]
    me = lax.axis_index(axis)

    def part(of):
        return lax.dynamic_index_in_dim(x, of, 0, keepdims=False)

    terms = [part(me)]
    for step in range(1, length):
        if length & (length - 1):
            pairs = [(i, (i + step) % length) for i in range(length)]
            to = lax.rem(me + step, length)
        else:
            pairs = [(i, i ^ step) for i in range(length)]
            to = me ^ step
        terms.append(lax.ppermute(part(to), axis, pairs))
    return terms


def shards(object_slab, probe_wave, amplitude, row_offset, col_offset, occupied):
    size = probe_wave.shape[1]
    rows, cols = object_slab.shape[1:]
    core = 1 - lax.axis_index("probe")
    narrow, wide, cores = (lax.axis_size(name) for name in ("narrow", "wide", "probe"))
    corner = jnp.stack([row_offset[0, 0, 0], col_offset[0, 0, 0]])
    here = [core, occupied[0, 0, 0], lax.axis_index("narrow")]
    here = jnp.stack([x.astype(jnp.int32) for x in here])
    scalars = jnp.concatenate([corner, here, swap(corner)])

    def shape(*dims, dtype=BF16):
        return jax.ShapeDtypeStruct(dims, dtype)

    cut = size // 2
    count = rows - cut
    start, more = call(
        first_rows, (shape(2, cut, cols), shape(2, count, cols)), [VMEM], 8, name="first_rows"
    )(object_slab)
    first = to_neighbour(start, -1, 0)
    second = to_neighbour(more, -1, 0)
    third = to_neighbour(first, -1, 1)
    late_scalars, first_late, late_probe, late_amplitude, late_tables = lax.optimization_barrier(
        (scalars, first, probe_wave, amplitude[0, 0, 0], dft_tables(size))
    )

    first2 = swap(first_late)
    width = size // (narrow * cores)
    table = shape(2, size, size)
    *tables, first_kept = call(
        functools.partial(shift_tables, width),
        (
            (table,) * 5
            + (shape(size, size), shape(size, size))
            + (shape(cols, narrow * width),) * 2
            + (shape(2, cut, cols),)
        ),
        [SMEM] + [VMEM] * 4 + [ANY],
        8,
        flops=0 * 10**9,
        name="shift_tables",
    )(late_scalars, late_tables, late_probe, late_amplitude, first_late, first2)
    second, tables = lax.optimization_barrier((second, tables))
    pieces = (first_kept, first2, second, swap(second), third, swap(third))
    blocks = shape(narrow, wide, 2, size // wide, width)
    *tables, back_rows, back_cols, back_cols2 = tables
    sent, kept, term = call(
        slot_terms,
        (shape(2, count, cols), shape(2, count, cols), table),
        [SMEM] + [VMEM] * 13,
        18,
        scratch=[pltpu.VMEM((2, size, size), BF16)] * 5
        + [pltpu.VMEM((2, rows, size), BF16)],
        flops=6 * 10**9,
        bytes_accessed=2 * 10**7,
        name="slot_terms",
    )(scalars, object_slab, *pieces, *tables)

    probe_sent, probe_kept = call(
        probe_parts, (blocks, blocks), [VMEM] * 4, 8, name="probe_parts"
    )(term, back_rows, back_cols, back_cols2)
    got, probe_got = swap(sent), swap(probe_sent)

    def tile(name, kernel, height, *more, after=()):
        return call(
            functools.partial(kernel, (rows, size), cut, len(after)),
            shape(2, height, cols),
            [SMEM] + [ANY] * len(after) + [VMEM] * (2 + len(more)),
            8,
            name=name,
        )(scalars, *after, kept, got, *more)

    def diag_part(dims, cut, skip, scalars, *refs):
        tile_part(dims, cut, 0, 0, scalars, *refs[skip:])

    def later_part(dims, cut, skip, scalars, *refs):
        tile_part(dims, cut, 1 - scalars[2], scalars[2], scalars, *refs[skip:])

    diag = tile("diag_part", diag_part, cut, after=(probe_sent,))
    from_first = to_neighbour(diag, 1, 0)
    probe_blocks = call(
        functools.partial(probe_sum, narrow),
        (jax.ShapeDtypeStruct(blocks.shape[1:], BF16),) * narrow,
        [SMEM, ANY, VMEM, VMEM],
        8,
        name="probe_sum",
    )(scalars, diag, probe_kept, probe_got)
    upper, lower = call(
        functools.partial(now_parts, (rows, size), cut),
        (shape(2, cut, cols), shape(2, count - cut, cols)),
        [SMEM, ANY, VMEM, VMEM],
        8,
        name="now_parts",
    )(scalars, probe_blocks[0], kept, got)
    from_upper = to_neighbour(upper, 1, 0)
    from_lower = to_neighbour(lower, 1, 0, senders=(1,))
    from_third = to_neighbour(tile("later_part", later_part, cut, from_first), 1, 1)
    received = [
        lax.ppermute(block, "narrow", [(i, (i + step) % narrow) for i in range(narrow)])
        for step, block in enumerate(probe_blocks)
        if step
    ]
    total = sum_of(probe_blocks[0], *received)
    terms = scatter_parts(total, "wide")
    probe_grad = call(
        functools.partial(scaled_sum, 1.0 / math.sqrt(wide * narrow * cores)),
        jax.ShapeDtypeStruct(terms[0].shape, F32),
        [VMEM] * len(terms),
        8,
        flops=20 * 10**9,
        name="probe_grad",
    )(*terms)
    own = call(
        functools.partial(own_part, (rows, size), cut),
        shape(2, count, cols),
        [SMEM, ANY] + [VMEM] * 4,
        8,
        flops=1 * 10**9,
        name="own_part",
    )(scalars, total, kept, got, from_upper, from_lower)
    other, last, other_last = swap(own), from_third, swap(from_third)
    mine = own[:, :cut].astype(F32) + last.astype(F32)
    theirs = other[:, :cut].astype(F32) + other_last.astype(F32)
    object_grad = jnp.concatenate(
        [
            jnp.where(core == 0, mine, theirs).astype(BF16),
            jnp.where(core == 0, theirs, mine).astype(BF16),
            jnp.where(core == 0, other[:, cut:], own[:, cut:]),
        ],
        1,
    )
    return (object_grad, probe_grad)


def solution(mesh):
    in_specs = (
        P(None, ("groups", "narrow"), "wide"),
        P(),
        P(("groups", "narrow"), "wide", "probe", None, None),
        P(("groups", "narrow"), "wide", "probe"),
        P(("groups", "narrow"), "wide", "probe"),
        P(("groups", "narrow"), "wide", "probe"),
    )
    out_specs = (
        P(None, ("groups", "narrow"), "wide"),
        P(None, ("groups", "wide"), ("narrow", "probe")),
    )
    return jax.shard_map(shards, mesh=mesh, in_specs=in_specs, out_specs=out_specs, check_vma=False)
```

```python
import functools
import math

import jax
import jax.numpy as jnp
import numpy as np
from jax import lax
from jax.experimental import pallas as pl
from jax.experimental.pallas import tpu as pltpu
from jax.sharding import PartitionSpec as P

BF16 = jnp.bfloat16
F32 = jnp.float32
VMEM = pl.BlockSpec(memory_space=pltpu.VMEM)
SMEM = pl.BlockSpec(memory_space=pltpu.SMEM)
ANY = pl.BlockSpec(memory_space=pl.ANY)


def to_neighbour(x, by, along_narrow, senders=(0, 1)):
    wide, narrow, cores = (lax.axis_size(name) for name in ("wide", "narrow", "probe"))
    pairs = []
    for w in range(wide):
        for n in range(narrow):
            for role in senders:
                core = 1 - role
                w_to, n_to = (w, n + by) if role == along_narrow else (w + by, n)
                if 0 <= w_to < wide and 0 <= n_to < narrow:
                    source = (w * narrow + n) * cores + core
                    pairs.append((source, (w_to * narrow + n_to) * cores + core))
    return lax.ppermute(x, ("wide", "narrow", "probe"), pairs)


def swap(x):
    return lax.ppermute(x, "probe", [(0, 1), (1, 0)])


def halves_first(size):
    return np.concatenate([np.arange(0, size, 2), np.arange(1, size, 2)])


def dft_tables(size):
    product = (np.arange(size)[:, None] * halves_first(size)[None, :]) % size
    angle = product.astype(np.float32) * np.float32(2.0 * math.pi / size)
    norm = np.float32(1.0 / math.sqrt(size))
    pair = (np.cos(angle) * norm, -np.sin(angle) * norm)
    return jnp.asarray(np.stack(pair + tuple(x.T for x in pair)), BF16)


def dot(a, b):
    return jnp.dot(a, b, preferred_element_type=F32)


def iota(shape, dim):
    return lax.broadcasted_iota(jnp.int32, shape, dim)


def one_hot(equal):
    return jnp.where(equal, 1.0, 0.0).astype(BF16)


def cyclic(at, shift, period):
    back = at - shift
    return jnp.where(back < 0, back + period, back)


def call(kernel, out_shape, in_specs, vmem, scratch=(), flops=0, bytes_accessed=0, name=None):
    return pl.pallas_call(
        kernel,
        out_shape=out_shape,
        in_specs=in_specs,
        out_specs=jax.tree.map(lambda _: VMEM, out_shape),
        scratch_shapes=list(scratch),
        compiler_params=pltpu.CompilerParams(vmem_limit_bytes=vmem * 1024 * 1024),
        cost_estimate=pl.CostEstimate(
            flops=flops, bytes_accessed=bytes_accessed, transcendentals=0
        ),
        name=name,
    )


def shift_tables(
    width, scalars, dft, probe_in, amp_in, first_in, before,
    right, right_t, left_t, left, probe, amplitude, back_rows, back_cols, back_cols2, first,
):
    size = dft.shape[1]
    part = size // 2
    first[...] = first_in[...]
    row_start, col_start, core = scalars[0], scalars[1], scalars[2]
    row_start = jnp.where(row_start >= size, row_start - size, row_start)
    full = (size, size)

    back_rows[...] = one_hot(cyclic(iota(full, 1), row_start, size) == iota(full, 0))
    count = back_cols.shape[1]
    for out, owner in ((back_cols, 1 - core), (back_cols2, core)):
        at = iota((size, count), 1)
        column = at + (at // width + owner) * width
        out[...] = one_hot(cyclic(iota((size, count), 0), col_start, size) == column)

    for start, table, table_t in ((col_start, right, right_t), (row_start, left_t, left)):
        hot = one_hot(cyclic(iota((part, size), 0), start, size) == iota((part, size), 1))
        hot_t = one_hot(cyclic(iota((size, part), 1), start, size) == iota((size, part), 0))
        cos_part, sin_part = dot(hot, dft[0]), dot(hot, dft[1])
        cos_turn, sin_turn = dot(dft[2], hot_t), dot(dft[3], hot_t)
        for odd in range(2):
            at = slice(odd * part, (odd + 1) * part)
            table[odd, :part, :part] = cos_part[:, at].astype(BF16)
            table[odd, part:, part:] = cos_part[:, at].astype(BF16)
            table[odd, :part, part:] = sin_part[:, at].astype(BF16)
            table[odd, part:, :part] = (-sin_part[:, at]).astype(BF16)
            table_t[odd, :part, :part] = cos_turn[at].astype(BF16)
            table_t[odd, part:, part:] = cos_turn[at].astype(BF16)
            table_t[odd, part:, :part] = sin_turn[at].astype(BF16)
            table_t[odd, :part, part:] = (-sin_turn[at]).astype(BF16)

    row_hot = one_hot(cyclic(iota(full, 0), row_start, size) == iota(full, 1))
    col_hot_t = one_hot(cyclic(iota(full, 1), col_start, size) == iota(full, 0))
    for plane in range(2):
        moved = dot(row_hot, probe_in[plane]).astype(BF16)
        probe[plane] = dot(moved, col_hot_t).astype(BF16)

    def frequency(at):
        return jnp.where(at < part, 2 * at, 2 * at - (size - 1))

    moved = dot(one_hot(frequency(iota(full, 0)) == iota(full, 1)), amp_in[...]).astype(BF16)
    amplitude[...] = dot(moved, one_hot(frequency(iota(full, 1)) == iota(full, 0))).astype(BF16)


def first_rows(slab, out, second):
    core = 1 - lax.axis_index("probe")
    count = out.shape[1]
    out[...] = slab[:, pl.ds(pl.multiple_of(count * (1 - core), 128), count)]
    second[...] = slab[:, pl.ds(pl.multiple_of(count * core, 128), second.shape[1])]


def slot_terms(
    scalars, own, first, first2, second, second2, third, third2,
    right, right_t, left_t, left, probe, amplitude,
    sent, kept, term, exit_wave, half, chi, back_half, patch, obj,
):
    rows, size = own.shape[1:]
    cut = first.shape[1]
    part = size // 2
    row_start, col_start, core = scalars[0], scalars[1], scalars[2]
    live = scalars[3].astype(F32)
    step = 128
    in_cols = iota((step, size), 1) >= col_start

    def tile_value(on, plane, row):
        def load(on_core_0, on_core_1, at):
            return (on_core_1 if on else on_core_0)[plane, pl.ds(at, step)].astype(F32)

        if row < rows:
            here = own[plane, pl.ds(row, step)].astype(F32)
            side = load(first2, first, row) if row < cut else load(second2, second, row - cut)
        elif row - rows < cut:
            here = load(second, second2, row - rows)
            side = load(third2, third, row - rows)
        else:
            here = load(first, first2, row - rows - cut)
            side = load(third, third2, row - rows - cut)
        return jnp.where(in_cols, here, side)

    def assemble(on):
        for start in range(0, size, step):
            at = pl.ds(start, step)
            planes = []
            for plane in range(2):
                row = start
                while row < rows:
                    row += size
                value = tile_value(on, plane, row)
                while row > start:
                    row -= size
                    in_rows = iota((step, size), 0) + row >= row_start
                    value = jnp.where(in_rows, tile_value(on, plane, row), value)
                patch[plane, at] = value.astype(BF16)
                planes.append(value)
            probe_re, probe_im = probe[0, at].astype(F32), probe[1, at].astype(F32)
            exit_re = probe_re * planes[0] - probe_im * planes[1]
            exit_im = probe_re * planes[1] + probe_im * planes[0]
            for plane, value in ((0, exit_re), (1, exit_im)):
                where = slice(plane * part, (plane + 1) * part)
                exit_wave[0, at, where] = (value[:, :part] + value[:, part:]).astype(BF16)
                exit_wave[1, at, where] = (value[:, :part] - value[:, part:]).astype(BF16)

    for on in range(2):
        pl.when(core == on)(functools.partial(assemble, on))

    for odd in range(2):
        result = dot(exit_wave[odd], right[odd])
        cols = slice(odd * part, (odd + 1) * part)
        for plane in range(2):
            where = slice(plane * part, (plane + 1) * part)
            low, high = result[:part, where], result[part:, where]
            half[0, where, cols] = (low + high).astype(BF16)
            half[1, where, cols] = (low - high).astype(BF16)
    for odd in range(2):
        far = dot(left[odd], half[odd])
        far_re, far_im = far[:part], far[part:]
        magnitude = jnp.sqrt(far_re * far_re + far_im * far_im)
        at = slice(odd * part, (odd + 1) * part)
        factor = (1.0 - amplitude[at].astype(F32) / jnp.maximum(magnitude, 1.0)) * live
        for plane, value in ((0, far_re * factor), (1, far_im * factor)):
            where = slice(plane * part, (plane + 1) * part)
            chi[0, at, where] = value[:, :part].astype(BF16)
            chi[1, at, where] = value[:, part:].astype(BF16)
    for plane in range(2):
        where = slice(plane * part, (plane + 1) * part)
        even, odd = dot(chi[0], right_t[0, :, where]), dot(chi[1], right_t[1, :, where])
        for parity in range(2):
            at = slice(parity * part, (parity + 1) * part)
            back_half[parity, where, :part] = (even[at] + odd[at]).astype(BF16)
            back_half[parity, where, part:] = (even[at] - odd[at]).astype(BF16)
    for start in range(0, size, part):
        at = slice(start, start + part)
        even, odd = dot(left_t[0], back_half[0, :, at]), dot(left_t[1], back_half[1, :, at])
        for lines, back in ((slice(0, part), even + odd), (slice(part, size), even - odd)):
            back_re, back_im = back[:part], back[part:]
            probe_re, probe_im = probe[0, lines, at].astype(F32), probe[1, lines, at].astype(F32)
            obj[0, lines, at] = (probe_re * back_re + probe_im * back_im).astype(BF16)
            obj[1, lines, at] = (probe_re * back_im - probe_im * back_re).astype(BF16)
            patch_re, patch_im = patch[0, lines, at].astype(F32), patch[1, lines, at].astype(F32)
            term[0, lines, at] = (patch_re * back_re + patch_im * back_im).astype(BF16)
            term[1, lines, at] = (patch_re * back_im - patch_im * back_re).astype(BF16)
    count = kept.shape[1]
    for plane in range(2):
        obj[plane, size:] = obj[plane, : obj.shape[1] - size]
        kept[plane] = obj[plane, pl.ds(pl.multiple_of(cut * core, 128), count)]
        sent[plane] = obj[plane, pl.ds(pl.multiple_of(cut * (1 - core), 128), count)]


def probe_parts(term, back_rows, back_cols, back_cols2, probe_sent, probe_kept):
    narrow, blocks, _, height, width = probe_sent.shape
    for plane in range(2):
        moved = dot(back_rows[...], term[plane]).astype(BF16)
        for out, hot in ((probe_sent, back_cols2), (probe_kept, back_cols)):
            result = dot(moved, hot[...]).astype(BF16)
            for column in range(narrow):
                for row in range(blocks):
                    out[column, row, plane] = result[
                        row * height : (row + 1) * height, column * width : (column + 1) * width
                    ]


def part_of(scalars, kept, got, shape, cut, start, rows_in, cols_in):
    rows, size = shape
    step, cols = 128, kept.shape[2]
    below = (1 - rows_in) * (rows - size)
    at = pl.ds(start + below if isinstance(below, int) else pl.multiple_of(start + below, 128), step)
    row_at = iota((step, cols), 0) + (scalars[2] * cut + start + (1 - rows_in) * rows)
    col_at = iota((step, cols), 1)
    masks = []
    for row_start, col_start in ((scalars[0], scalars[1]), (scalars[5], scalars[6])):
        in_cols = jnp.where(col_at >= col_start, 1, 0) == cols_in
        masks.append((row_at >= row_start) & (row_at < row_start + size) & in_cols)
    return [
        jnp.where(masks[0], kept[plane, at].astype(F32), 0.0)
        + jnp.where(masks[1], got[plane, at].astype(F32), 0.0)
        for plane in range(2)
    ]


def tile_part(shape, cut, rows_in, cols_in, scalars, kept, got, *refs):
    *arrived, out = refs
    fill(shape, cut, 0, rows_in, cols_in, scalars, kept, got, arrived, out)


def fill(shape, cut, first, rows_in, cols_in, scalars, kept, got, arrived, out):
    step = 128
    for start in range(0, out.shape[1], step):
        at = pl.ds(start, step)
        part = part_of(scalars, kept, got, shape, cut, first + start, rows_in, cols_in)
        for plane in range(2):
            for more in arrived:
                part[plane] = part[plane] + more[plane, at].astype(F32)
            out[plane, at] = part[plane].astype(BF16)


def now_parts(shape, cut, scalars, before, kept, got, upper, lower):
    core = scalars[2]
    fill(shape, cut, 0, core, 1 - core, scalars, kept, got, (), upper)
    fill(shape, cut, cut, 1, 0, scalars, kept, got, (), lower)


def own_part(shape, cut, scalars, before, kept, got, upper, lower, out):
    fill(shape, cut, 0, 1, 1, scalars, kept, got, (upper,), out.at[:, :cut])
    fill(shape, cut, cut, 1, 1, scalars, kept, got, (lower,), out.at[:, cut:])


def probe_sum(narrow, scalars, diag, probe_kept, probe_got, *outs):
    me = scalars[4]
    for step, out in enumerate(outs):
        block = lax.rem(me + step, narrow)
        total = probe_kept[block].astype(F32) + probe_got[block].astype(F32)
        out[...] = total.astype(BF16)


def sum_kernel(*refs):
    *terms, out = refs
    total = terms[0][...].astype(F32)
    for term in terms[1:]:
        total = total + term[...].astype(F32)
    out[...] = total.astype(out.dtype)


def scaled_sum(scale, *refs):
    *terms, out = refs
    sum_kernel(*terms, out)
    out[...] = out[...] * scale


def sum_of(*terms):
    return call(
        sum_kernel,
        jax.ShapeDtypeStruct(terms[0].shape, BF16),
        [VMEM] * len(terms),
        8,
        flops=8 * 10**9,
        name="sum",
    )(*terms)


def scatter_parts(x, axis):
    length = lax.axis_size(axis)
    if length > 8:
        return [lax.psum_scatter(x, axis, scatter_dimension=0, tiled=True)[0]]
    me = lax.axis_index(axis)

    def part(of):
        return lax.dynamic_index_in_dim(x, of, 0, keepdims=False)

    terms = [part(me)]
    for step in range(1, length):
        if length & (length - 1):
            pairs = [(i, (i + step) % length) for i in range(length)]
            to = lax.rem(me + step, length)
        else:
            pairs = [(i, i ^ step) for i in range(length)]
            to = me ^ step
        terms.append(lax.ppermute(part(to), axis, pairs))
    return terms


def shards(object_slab, probe_wave, amplitude, row_offset, col_offset, occupied):
    size = probe_wave.shape[1]
    rows, cols = object_slab.shape[1:]
    core = 1 - lax.axis_index("probe")
    narrow, wide, cores = (lax.axis_size(name) for name in ("narrow", "wide", "probe"))
    corner = jnp.stack([row_offset[0, 0, 0], col_offset[0, 0, 0]])
    here = [core, occupied[0, 0, 0], lax.axis_index("narrow")]
    here = jnp.stack([x.astype(jnp.int32) for x in here])
    scalars = jnp.concatenate([corner, here, swap(corner)])

    def shape(*dims, dtype=BF16):
        return jax.ShapeDtypeStruct(dims, dtype)

    cut = size // 2
    count = rows - cut
    start, more = call(
        first_rows, (shape(2, cut, cols), shape(2, count, cols)), [VMEM], 8, name="first_rows"
    )(object_slab)
    first = to_neighbour(start, -1, 0)
    second = to_neighbour(more, -1, 0)
    third = to_neighbour(first, -1, 1)
    late_scalars, first_late, late_probe, late_amplitude, late_tables = lax.optimization_barrier(
        (scalars, first, probe_wave, amplitude[0, 0, 0], dft_tables(size))
    )

    first2 = swap(first_late)
    width = size // (narrow * cores)
    table = shape(2, size, size)
    *tables, first_kept = call(
        functools.partial(shift_tables, width),
        (
            (table,) * 5
            + (shape(size, size), shape(size, size))
            + (shape(cols, narrow * width),) * 2
            + (shape(2, cut, cols),)
        ),
        [SMEM] + [VMEM] * 4 + [ANY],
        8,
        flops=0 * 10**9,
        name="shift_tables",
    )(late_scalars, late_tables, late_probe, late_amplitude, first_late, first2)
    second, tables = lax.optimization_barrier((second, tables))
    pieces = (first_kept, first2, second, swap(second), third, swap(third))
    blocks = shape(narrow, wide, 2, size // wide, width)
    *tables, back_rows, back_cols, back_cols2 = tables
    sent, kept, term = call(
        slot_terms,
        (shape(2, count, cols), shape(2, count, cols), table),
        [SMEM] + [VMEM] * 13,
        18,
        scratch=[pltpu.VMEM((2, size, size), BF16)] * 5
        + [pltpu.VMEM((2, rows, size), BF16)],
        flops=6 * 10**9,
        bytes_accessed=2 * 10**7,
        name="slot_terms",
    )(scalars, object_slab, *pieces, *tables)

    probe_sent, probe_kept = call(
        probe_parts, (blocks, blocks), [VMEM] * 4, 8, name="probe_parts"
    )(term, back_rows, back_cols, back_cols2)
    got, probe_got = swap(sent), swap(probe_sent)

    def tile(name, kernel, height, *more, after=()):
        return call(
            functools.partial(kernel, (rows, size), cut, len(after)),
            shape(2, height, cols),
            [SMEM] + [ANY] * len(after) + [VMEM] * (2 + len(more)),
            8,
            name=name,
        )(scalars, *after, kept, got, *more)

    def diag_part(dims, cut, skip, scalars, *refs):
        tile_part(dims, cut, 0, 0, scalars, *refs[skip:])

    def later_part(dims, cut, skip, scalars, *refs):
        tile_part(dims, cut, 1 - scalars[2], scalars[2], scalars, *refs[skip:])

    diag = tile("diag_part", diag_part, cut, after=(probe_sent,))
    from_first = to_neighbour(diag, 1, 0)
    probe_blocks = call(
        functools.partial(probe_sum, narrow),
        (jax.ShapeDtypeStruct(blocks.shape[1:], BF16),) * narrow,
        [SMEM, ANY, VMEM, VMEM],
        8,
        name="probe_sum",
    )(scalars, diag, probe_kept, probe_got)
    upper, lower = call(
        functools.partial(now_parts, (rows, size), cut),
        (shape(2, cut, cols), shape(2, count - cut, cols)),
        [SMEM, ANY, VMEM, VMEM],
        8,
        name="now_parts",
    )(scalars, probe_blocks[0], kept, got)
    from_upper = to_neighbour(upper, 1, 0)
    from_lower = to_neighbour(lower, 1, 0, senders=(1,))
    from_third = to_neighbour(tile("later_part", later_part, cut, from_first), 1, 1)
    received = [
        lax.ppermute(block, "narrow", [(i, (i + step) % narrow) for i in range(narrow)])
        for step, block in enumerate(probe_blocks)
        if step
    ]
    total = sum_of(probe_blocks[0], *received)
    terms = scatter_parts(total, "wide")
    probe_grad = call(
        functools.partial(scaled_sum, 1.0 / math.sqrt(wide * narrow * cores)),
        jax.ShapeDtypeStruct(terms[0].shape, F32),
        [VMEM] * len(terms),
        8,
        flops=20 * 10**9,
        name="probe_grad",
    )(*terms)
    own = call(
        functools.partial(own_part, (rows, size), cut),
        shape(2, count, cols),
        [SMEM, ANY] + [VMEM] * 4,
        8,
        flops=1 * 10**9,
        name="own_part",
    )(scalars, total, kept, got, from_upper, from_lower)
    other, last, other_last = swap(own), from_third, swap(from_third)
    mine = own[:, :cut].astype(F32) + last.astype(F32)
    theirs = other[:, :cut].astype(F32) + other_last.astype(F32)
    object_grad = jnp.concatenate(
        [
            jnp.where(core == 0, mine, theirs).astype(BF16),
            jnp.where(core == 0, theirs, mine).astype(BF16),
            jnp.where(core == 0, other[:, cut:], own[:, cut:]),
        ],
        1,
    )
    return (object_grad, probe_grad)


def solution(mesh):
    in_specs = (
        P(None, ("groups", "narrow"), "wide"),
        P(),
        P(("groups", "narrow"), "wide", "probe", None, None),
        P(("groups", "narrow"), "wide", "probe"),
        P(("groups", "narrow"), "wide", "probe"),
        P(("groups", "narrow"), "wide", "probe"),
    )
    out_specs = (
        P(None, ("groups", "narrow"), "wide"),
        P(None, ("groups", "wide"), ("narrow", "probe")),
    )
    return jax.shard_map(shards, mesh=mesh, in_specs=in_specs, out_specs=out_specs, check_vma=False)
```

```python
import functools
import math

import jax
import jax.numpy as jnp
import numpy as np
from jax import lax
from jax.experimental import pallas as pl
from jax.experimental.pallas import tpu as pltpu
from jax.sharding import PartitionSpec as P

BF16 = jnp.bfloat16
F32 = jnp.float32
VMEM = pl.BlockSpec(memory_space=pltpu.VMEM)
SMEM = pl.BlockSpec(memory_space=pltpu.SMEM)
ANY = pl.BlockSpec(memory_space=pl.ANY)


def to_neighbour(x, by, along_narrow, senders=(0, 1)):
    wide, narrow, cores = (lax.axis_size(name) for name in ("wide", "narrow", "probe"))
    pairs = []
    for w in range(wide):
        for n in range(narrow):
            for role in senders:
                core = 1 - role
                w_to, n_to = (w, n + by) if role == along_narrow else (w + by, n)
                if 0 <= w_to < wide and 0 <= n_to < narrow:
                    source = (w * narrow + n) * cores + core
                    pairs.append((source, (w_to * narrow + n_to) * cores + core))
    return lax.ppermute(x, ("wide", "narrow", "probe"), pairs)


def swap(x):
    return lax.ppermute(x, "probe", [(0, 1), (1, 0)])


def halves_first(size):
    return np.concatenate([np.arange(0, size, 2), np.arange(1, size, 2)])


def dft_tables(size):
    product = (np.arange(size)[:, None] * halves_first(size)[None, :]) % size
    angle = product.astype(np.float32) * np.float32(2.0 * math.pi / size)
    norm = np.float32(1.0 / math.sqrt(size))
    pair = (np.cos(angle) * norm, -np.sin(angle) * norm)
    return jnp.asarray(np.stack(pair + tuple(x.T for x in pair)), BF16)


def dot(a, b):
    return jnp.dot(a, b, preferred_element_type=F32)


def iota(shape, dim):
    return lax.broadcasted_iota(jnp.int32, shape, dim)


def one_hot(equal):
    return jnp.where(equal, 1.0, 0.0).astype(BF16)


def cyclic(at, shift, period):
    back = at - shift
    return jnp.where(back < 0, back + period, back)


def call(kernel, out_shape, in_specs, vmem, scratch=(), flops=0, bytes_accessed=0, name=None):
    return pl.pallas_call(
        kernel,
        out_shape=out_shape,
        in_specs=in_specs,
        out_specs=jax.tree.map(lambda _: VMEM, out_shape),
        scratch_shapes=list(scratch),
        compiler_params=pltpu.CompilerParams(vmem_limit_bytes=vmem * 1024 * 1024),
        cost_estimate=pl.CostEstimate(
            flops=flops, bytes_accessed=bytes_accessed, transcendentals=0
        ),
        name=name,
    )


def shift_tables(
    width, scalars, dft, probe_in, amp_in, first_in, before,
    right, right_t, left_t, left, probe, amplitude, back_rows, back_cols, back_cols2, first,
):
    size = dft.shape[1]
    part = size // 2
    first[...] = first_in[...]
    row_start, col_start, core = scalars[0], scalars[1], scalars[2]
    row_start = jnp.where(row_start >= size, row_start - size, row_start)
    full = (size, size)

    back_rows[...] = one_hot(cyclic(iota(full, 1), row_start, size) == iota(full, 0))
    count = back_cols.shape[1]
    for out, owner in ((back_cols, 1 - core), (back_cols2, core)):
        at = iota((size, count), 1)
        column = at + (at // width + owner) * width
        out[...] = one_hot(cyclic(iota((size, count), 0), col_start, size) == column)

    for start, table, table_t in ((col_start, right, right_t), (row_start, left_t, left)):
        hot = one_hot(cyclic(iota((part, size), 0), start, size) == iota((part, size), 1))
        hot_t = one_hot(cyclic(iota((size, part), 1), start, size) == iota((size, part), 0))
        cos_part, sin_part = dot(hot, dft[0]), dot(hot, dft[1])
        cos_turn, sin_turn = dot(dft[2], hot_t), dot(dft[3], hot_t)
        for odd in range(2):
            at = slice(odd * part, (odd + 1) * part)
            table[odd, :part, :part] = cos_part[:, at].astype(BF16)
            table[odd, part:, part:] = cos_part[:, at].astype(BF16)
            table[odd, :part, part:] = sin_part[:, at].astype(BF16)
            table[odd, part:, :part] = (-sin_part[:, at]).astype(BF16)
            table_t[odd, :part, :part] = cos_turn[at].astype(BF16)
            table_t[odd, part:, part:] = cos_turn[at].astype(BF16)
            table_t[odd, part:, :part] = sin_turn[at].astype(BF16)
            table_t[odd, :part, part:] = (-sin_turn[at]).astype(BF16)

    row_hot = one_hot(cyclic(iota(full, 0), row_start, size) == iota(full, 1))
    col_hot_t = one_hot(cyclic(iota(full, 1), col_start, size) == iota(full, 0))
    for plane in range(2):
        moved = dot(row_hot, probe_in[plane]).astype(BF16)
        probe[plane] = dot(moved, col_hot_t).astype(BF16)

    def frequency(at):
        return jnp.where(at < part, 2 * at, 2 * at - (size - 1))

    moved = dot(one_hot(frequency(iota(full, 0)) == iota(full, 1)), amp_in[...]).astype(BF16)
    amplitude[...] = dot(moved, one_hot(frequency(iota(full, 1)) == iota(full, 0))).astype(BF16)


def first_rows(slab, out, second):
    core = 1 - lax.axis_index("probe")
    count = out.shape[1]
    out[...] = slab[:, pl.ds(pl.multiple_of(count * (1 - core), 128), count)]
    second[...] = slab[:, pl.ds(pl.multiple_of(count * core, 128), second.shape[1])]


def slot_terms(
    scalars, own, first, first2, second, second2, third, third2,
    right, right_t, left_t, left, probe, amplitude,
    sent, kept, term, exit_wave, half, chi, back_half, patch, obj,
):
    rows, size = own.shape[1:]
    cut = first.shape[1]
    part = size // 2
    row_start, col_start, core = scalars[0], scalars[1], scalars[2]
    live = scalars[3].astype(F32)
    step = 128
    in_cols = iota((step, size), 1) >= col_start
    core_0 = iota((step, size), 0) * 0 + core == 0

    def tile_value(plane, row):
        def load(on_core_0, on_core_1, at):
            a, b = on_core_0[plane, pl.ds(at, step)], on_core_1[plane, pl.ds(at, step)]
            return jnp.where(core_0, a.astype(F32), b.astype(F32))

        if row < rows:
            here = own[plane, pl.ds(row, step)].astype(F32)
            side = load(first2, first, row) if row < cut else load(second2, second, row - cut)
        elif row - rows < cut:
            here = load(second, second2, row - rows)
            side = load(third2, third, row - rows)
        else:
            here = load(first, first2, row - rows - cut)
            side = load(third, third2, row - rows - cut)
        return jnp.where(in_cols, here, side)

    for start in range(0, size, step):
        at = pl.ds(start, step)
        planes = []
        for plane in range(2):
            row = start
            while row < rows:
                row += size
            value = tile_value(plane, row)
            while row > start:
                row -= size
                in_rows = iota((step, size), 0) + row >= row_start
                value = jnp.where(in_rows, tile_value(plane, row), value)
            patch[plane, at] = value.astype(BF16)
            planes.append(value)
        probe_re, probe_im = probe[0, at].astype(F32), probe[1, at].astype(F32)
        exit_re = probe_re * planes[0] - probe_im * planes[1]
        exit_im = probe_re * planes[1] + probe_im * planes[0]
        for plane, value in ((0, exit_re), (1, exit_im)):
            where = slice(plane * part, (plane + 1) * part)
            exit_wave[0, at, where] = (value[:, :part] + value[:, part:]).astype(BF16)
            exit_wave[1, at, where] = (value[:, :part] - value[:, part:]).astype(BF16)

    for odd in range(2):
        result = dot(exit_wave[odd], right[odd])
        cols = slice(odd * part, (odd + 1) * part)
        for plane in range(2):
            where = slice(plane * part, (plane + 1) * part)
            low, high = result[:part, where], result[part:, where]
            half[0, where, cols] = (low + high).astype(BF16)
            half[1, where, cols] = (low - high).astype(BF16)
    for odd in range(2):
        far = dot(left[odd], half[odd])
        far_re, far_im = far[:part], far[part:]
        magnitude = jnp.sqrt(far_re * far_re + far_im * far_im)
        at = slice(odd * part, (odd + 1) * part)
        factor = (1.0 - amplitude[at].astype(F32) / jnp.maximum(magnitude, 1.0)) * live
        for plane, value in ((0, far_re * factor), (1, far_im * factor)):
            where = slice(plane * part, (plane + 1) * part)
            chi[0, at, where] = value[:, :part].astype(BF16)
            chi[1, at, where] = value[:, part:].astype(BF16)
    for plane in range(2):
        where = slice(plane * part, (plane + 1) * part)
        even, odd = dot(chi[0], right_t[0, :, where]), dot(chi[1], right_t[1, :, where])
        for parity in range(2):
            at = slice(parity * part, (parity + 1) * part)
            back_half[parity, where, :part] = (even[at] + odd[at]).astype(BF16)
            back_half[parity, where, part:] = (even[at] - odd[at]).astype(BF16)
    for start in range(0, size, part):
        at = slice(start, start + part)
        even, odd = dot(left_t[0], back_half[0, :, at]), dot(left_t[1], back_half[1, :, at])
        for lines, back in ((slice(0, part), even + odd), (slice(part, size), even - odd)):
            back_re, back_im = back[:part], back[part:]
            probe_re, probe_im = probe[0, lines, at].astype(F32), probe[1, lines, at].astype(F32)
            obj[0, lines, at] = (probe_re * back_re + probe_im * back_im).astype(BF16)
            obj[1, lines, at] = (probe_re * back_im - probe_im * back_re).astype(BF16)
            patch_re, patch_im = patch[0, lines, at].astype(F32), patch[1, lines, at].astype(F32)
            term[0, lines, at] = (patch_re * back_re + patch_im * back_im).astype(BF16)
            term[1, lines, at] = (patch_re * back_im - patch_im * back_re).astype(BF16)
    count = kept.shape[1]
    for plane in range(2):
        obj[plane, size:] = obj[plane, : obj.shape[1] - size]
        kept[plane] = obj[plane, pl.ds(pl.multiple_of(cut * core, 128), count)]
        sent[plane] = obj[plane, pl.ds(pl.multiple_of(cut * (1 - core), 128), count)]


def probe_parts(term, back_rows, back_cols, back_cols2, probe_sent, probe_kept):
    narrow, blocks, _, height, width = probe_sent.shape
    for plane in range(2):
        moved = dot(back_rows[...], term[plane]).astype(BF16)
        for out, hot in ((probe_sent, back_cols2), (probe_kept, back_cols)):
            result = dot(moved, hot[...]).astype(BF16)
            for column in range(narrow):
                for row in range(blocks):
                    out[column, row, plane] = result[
                        row * height : (row + 1) * height, column * width : (column + 1) * width
                    ]


def part_of(scalars, kept, got, shape, cut, start, rows_in, cols_in):
    rows, size = shape
    step, cols = 128, kept.shape[2]
    below = (1 - rows_in) * (rows - size)
    at = pl.ds(start + below if isinstance(below, int) else pl.multiple_of(start + below, 128), step)
    row_at = iota((step, cols), 0) + (scalars[2] * cut + start + (1 - rows_in) * rows)
    col_at = iota((step, cols), 1)
    masks = []
    for row_start, col_start in ((scalars[0], scalars[1]), (scalars[5], scalars[6])):
        in_cols = jnp.where(col_at >= col_start, 1, 0) == cols_in
        masks.append((row_at >= row_start) & (row_at < row_start + size) & in_cols)
    return [
        jnp.where(masks[0], kept[plane, at].astype(F32), 0.0)
        + jnp.where(masks[1], got[plane, at].astype(F32), 0.0)
        for plane in range(2)
    ]


def tile_part(shape, cut, rows_in, cols_in, scalars, kept, got, *refs):
    *arrived, out = refs
    fill(shape, cut, 0, rows_in, cols_in, scalars, kept, got, arrived, out)


def fill(shape, cut, first, rows_in, cols_in, scalars, kept, got, arrived, out):
    step = 128
    for start in range(0, out.shape[1], step):
        at = pl.ds(start, step)
        part = part_of(scalars, kept, got, shape, cut, first + start, rows_in, cols_in)
        for plane in range(2):
            for more in arrived:
                part[plane] = part[plane] + more[plane, at].astype(F32)
            out[plane, at] = part[plane].astype(BF16)


def now_parts(shape, cut, scalars, before, kept, got, upper, lower):
    core = scalars[2]
    fill(shape, cut, 0, core, 1 - core, scalars, kept, got, (), upper)
    fill(shape, cut, cut, 1, 0, scalars, kept, got, (), lower)


def own_part(shape, cut, scalars, before, kept, got, upper, lower, out):
    fill(shape, cut, 0, 1, 1, scalars, kept, got, (upper,), out.at[:, :cut])
    fill(shape, cut, cut, 1, 1, scalars, kept, got, (lower,), out.at[:, cut:])


def probe_sum(narrow, scalars, diag, probe_kept, probe_got, *outs):
    me = scalars[4]
    for step, out in enumerate(outs):
        block = lax.rem(me + step, narrow)
        total = probe_kept[block].astype(F32) + probe_got[block].astype(F32)
        out[...] = total.astype(BF16)


def sum_kernel(*refs):
    *terms, out = refs
    total = terms[0][...].astype(F32)
    for term in terms[1:]:
        total = total + term[...].astype(F32)
    out[...] = total.astype(out.dtype)


def scaled_sum(scale, *refs):
    *terms, out = refs
    sum_kernel(*terms, out)
    out[...] = out[...] * scale


def sum_of(*terms):
    return call(
        sum_kernel,
        jax.ShapeDtypeStruct(terms[0].shape, BF16),
        [VMEM] * len(terms),
        8,
        flops=8 * 10**9,
        name="sum",
    )(*terms)


def scatter_parts(x, axis):
    length = lax.axis_size(axis)
    if length > 8:
        return [lax.psum_scatter(x, axis, scatter_dimension=0, tiled=True)[0]]
    me = lax.axis_index(axis)

    def part(of):
        return lax.dynamic_index_in_dim(x, of, 0, keepdims=False)

    terms = [part(me)]
    for step in range(1, length):
        if length & (length - 1):
            pairs = [(i, (i + step) % length) for i in range(length)]
            to = lax.rem(me + step, length)
        else:
            pairs = [(i, i ^ step) for i in range(length)]
            to = me ^ step
        terms.append(lax.ppermute(part(to), axis, pairs))
    return terms


def shards(object_slab, probe_wave, amplitude, row_offset, col_offset, occupied):
    size = probe_wave.shape[1]
    rows, cols = object_slab.shape[1:]
    core = 1 - lax.axis_index("probe")
    narrow, wide, cores = (lax.axis_size(name) for name in ("narrow", "wide", "probe"))
    corner = jnp.stack([row_offset[0, 0, 0], col_offset[0, 0, 0]])
    here = [core, occupied[0, 0, 0], lax.axis_index("narrow")]
    here = jnp.stack([x.astype(jnp.int32) for x in here])
    scalars = jnp.concatenate([corner, here, swap(corner)])

    def shape(*dims, dtype=BF16):
        return jax.ShapeDtypeStruct(dims, dtype)

    cut = size // 2
    count = rows - cut
    start, more = call(
        first_rows, (shape(2, cut, cols), shape(2, count, cols)), [VMEM], 8, name="first_rows"
    )(object_slab)
    first = to_neighbour(start, -1, 0)
    second = to_neighbour(more, -1, 0)
    third = to_neighbour(first, -1, 1)
    late_scalars, first_late, late_probe, late_amplitude, late_tables = lax.optimization_barrier(
        (scalars, first, probe_wave, amplitude[0, 0, 0], dft_tables(size))
    )

    first2 = swap(first_late)
    width = size // (narrow * cores)
    table = shape(2, size, size)
    *tables, first_kept = call(
        functools.partial(shift_tables, width),
        (
            (table,) * 5
            + (shape(size, size), shape(size, size))
            + (shape(cols, narrow * width),) * 2
            + (shape(2, cut, cols),)
        ),
        [SMEM] + [VMEM] * 4 + [ANY],
        8,
        flops=0 * 10**9,
        name="shift_tables",
    )(late_scalars, late_tables, late_probe, late_amplitude, first_late, first2)
    second, tables = lax.optimization_barrier((second, tables))
    pieces = (first_kept, first2, second, swap(second), third, swap(third))
    blocks = shape(narrow, wide, 2, size // wide, width)
    *tables, back_rows, back_cols, back_cols2 = tables
    sent, kept, term = call(
        slot_terms,
        (shape(2, count, cols), shape(2, count, cols), table),
        [SMEM] + [VMEM] * 13,
        24,
        scratch=[pltpu.VMEM((2, size, size), BF16)] * 5
        + [pltpu.VMEM((2, rows, size), BF16)],
        flops=6 * 10**9,
        bytes_accessed=2 * 10**7,
        name="slot_terms",
    )(scalars, object_slab, *pieces, *tables)

    probe_sent, probe_kept = call(
        probe_parts, (blocks, blocks), [VMEM] * 4, 8, name="probe_parts"
    )(term, back_rows, back_cols, back_cols2)
    got, probe_got = swap(sent), swap(probe_sent)

    def tile(name, kernel, height, *more, after=()):
        return call(
            functools.partial(kernel, (rows, size), cut, len(after)),
            shape(2, height, cols),
            [SMEM] + [ANY] * len(after) + [VMEM] * (2 + len(more)),
            8,
            name=name,
        )(scalars, *after, kept, got, *more)

    def diag_part(dims, cut, skip, scalars, *refs):
        tile_part(dims, cut, 0, 0, scalars, *refs[skip:])

    def later_part(dims, cut, skip, scalars, *refs):
        tile_part(dims, cut, 1 - scalars[2], scalars[2], scalars, *refs[skip:])

    diag = tile("diag_part", diag_part, cut, after=(probe_sent,))
    from_first = to_neighbour(diag, 1, 0)
    probe_blocks = call(
        functools.partial(probe_sum, narrow),
        (jax.ShapeDtypeStruct(blocks.shape[1:], BF16),) * narrow,
        [SMEM, ANY, VMEM, VMEM],
        8,
        name="probe_sum",
    )(scalars, diag, probe_kept, probe_got)
    upper, lower = call(
        functools.partial(now_parts, (rows, size), cut),
        (shape(2, cut, cols), shape(2, count - cut, cols)),
        [SMEM, ANY, VMEM, VMEM],
        8,
        name="now_parts",
    )(scalars, probe_blocks[0], kept, got)
    from_upper = to_neighbour(upper, 1, 0)
    from_lower = to_neighbour(lower, 1, 0, senders=(1,))
    from_third = to_neighbour(tile("later_part", later_part, cut, from_first), 1, 1)
    received = [
        lax.ppermute(block, "narrow", [(i, (i + step) % narrow) for i in range(narrow)])
        for step, block in enumerate(probe_blocks)
        if step
    ]
    total = sum_of(probe_blocks[0], *received)
    terms = scatter_parts(total, "wide")
    probe_grad = call(
        functools.partial(scaled_sum, 1.0 / math.sqrt(wide * narrow * cores)),
        jax.ShapeDtypeStruct(terms[0].shape, F32),
        [VMEM] * len(terms),
        8,
        flops=20 * 10**9,
        name="probe_grad",
    )(*terms)
    own = call(
        functools.partial(own_part, (rows, size), cut),
        shape(2, count, cols),
        [SMEM, ANY] + [VMEM] * 4,
        8,
        flops=1 * 10**9,
        name="own_part",
    )(scalars, total, kept, got, from_upper, from_lower)
    other, last, other_last = swap(own), from_third, swap(from_third)
    mine = own[:, :cut].astype(F32) + last.astype(F32)
    theirs = other[:, :cut].astype(F32) + other_last.astype(F32)
    object_grad = jnp.concatenate(
        [
            jnp.where(core == 0, mine, theirs).astype(BF16),
            jnp.where(core == 0, theirs, mine).astype(BF16),
            jnp.where(core == 0, other[:, cut:], own[:, cut:]),
        ],
        1,
    )
    return (object_grad, probe_grad)


def solution(mesh):
    in_specs = (
        P(None, ("groups", "narrow"), "wide"),
        P(),
        P(("groups", "narrow"), "wide", "probe", None, None),
        P(("groups", "narrow"), "wide", "probe"),
        P(("groups", "narrow"), "wide", "probe"),
        P(("groups", "narrow"), "wide", "probe"),
    )
    out_specs = (
        P(None, ("groups", "narrow"), "wide"),
        P(None, ("groups", "wide"), ("narrow", "probe")),
    )
    return jax.shard_map(shards, mesh=mesh, in_specs=in_specs, out_specs=out_specs, check_vma=False)
```
